32 devices in a mesh: groups: 2 (over x), patch: 16 (over z, y, core).
Axes of the slice: x: 2, y: 2, z: 4, core: 2. Of those that a mesh axis runs over, the one named last changes fastest.
Arguments:
- template: float32 [64, 32768], P(None, ('groups', 'patch')), parts along dimension 1, may hold values from -6 to 6
- science: float32 [512, 4, 128], P(('groups', 'patch')), parts along dimension 0, may hold values from -6 to 6
- dest: int32 [512, 1], P(('groups', 'patch')), parts along dimension 0, may hold values from 0 to 15; in each aligned block of 16 rows (0 to 15, 16 to 31, ...) at most 2 rows name the same one
- row_offset: int32 [512], P(('groups', 'patch')), parts along dimension 0, may hold values from 0 to 60
- col_block: int32 [512], P(('groups', 'patch')), parts along dimension 0, may hold values from 0 to 7
- basis_rows: float32 [27, 21], replicated, may hold values from -1.25 to 1.25
- basis_cols: float32 [27, 21], replicated, may hold values from -1.25 to 1.25
- stamp_rows: int32 [32, 24], P('groups'), parts along dimension 0, may hold values from 0 to 63
- stamp_cols: int32 [32, 24], P('groups'), parts along dimension 0, may hold values from 0 to 1023
Outputs:
- difference: float32 [512, 4, 128], P(('groups', 'patch')), parts along dimension 0
The draws below stay inside these ranges and needn't reach their ends.
There are 2 independent parts, one for each index of `groups`. The reference program is written for one: setup_inputs(seed, part) draws one part's arguments, and reference() takes and returns one part's arrays. A program takes and returns all parts, laid end to end along the dimension named above; an argument that names none is the same for every part. Nothing has to cross between parts.
Inputs may be any that keep to these rules, and one draw needn't show every extreme that they name: `dest`: each visit sends at most 2 strips to one sub-patch, and in every draw some visit sends exactly 2 to one.
All inputs are finite; a program needn't handle non-finite values.
Results may differ from the reference program's by a relative error of at most 0.0003.
Values sent between devices are 32-bit elements; how exact they have to be, the bound alone decides.
A program may use at most 64 MiB of HBM per device.

```python
import math
import jax
import jax.numpy as jnp
import numpy as np
from jax import lax

BASES = 27
TAPS = 21
BLOCK = 128
CAP = 2
STAMPS = 24
STAMP_HALF = 10
STRIP_ROWS = 4
SUB_ROWS = 64
SUB_COLS = 1024
STRIPS = 16
TOTAL_STRIPS = 256
N_PATCH = 16


def plant(values, stream_key, least, high):
    shape = values.shape
    spot = [jax.random.randint(jax.random.fold_in(stream_key, axis), (), 0, shape[axis]) for axis in range(len(shape))]
    values = values.at[tuple(spot)].set(least)
    longest = shape.index(max(shape))
    spot[longest] = (spot[longest] + 1) % shape[longest]
    return values.at[tuple(spot)].set(high)


def block_levels(rng, extent, shards, least, high):
    factor_of, own = 1.0, jax.random.fold_in(rng, 6)
    for axis_at, shards_of in shards:
        heights = jnp.exp(jax.random.uniform(jax.random.fold_in(own, axis_at), (shards_of,), jnp.float32, least / len(shards), high / len(shards)))
        factor_of = factor_of * jnp.repeat(heights, extent[axis_at] // shards_of).reshape([-1 if axis == axis_at else 1 for axis in range(len(extent))])
    return factor_of


def shared_out(stream_key, own, number, rows, amount, top, limit, slope):
    sequence = jax.random.permutation(stream_key, amount)
    packed, common = portions_of(amount, rows * top, limit, slope, True), portions_of(amount, rows * top, limit, slope, False)
    places = jnp.arange(amount)

    def named(lengths, rotation):
        used = int((lengths > 0).sum())
        fixed = max(1, used // 4)
        passed = fixed + (places - fixed + rotation * (used - fixed)) % max(1, amount - fixed)
        return jnp.zeros((amount,), jnp.int32).at[sequence[jnp.where(places < fixed, places, passed)]].set(jnp.asarray(lengths, jnp.int32))

    lengths = jnp.where(number % 4 == 0, named(packed, number // 4), named(common, number - number // 4 - 1))
    mixed = jax.random.permutation(jax.random.fold_in(own, 3), amount)
    donor, sink = mixed[0:amount // 2 * 2:2], mixed[1:amount // 2 * 2:2]
    slack = jnp.minimum(lengths[donor] - 1, limit - lengths[sink]) // 2
    slack = jnp.where((donor == sequence[0]) | (sink == sequence[0]) | (lengths[sink] == 0), 0, jnp.maximum(slack, 0))
    passed = jax.random.randint(jax.random.fold_in(own, 4), (amount // 2,), 0, 1 << 20) % (slack + 1)
    lengths = lengths.at[donor].add(-passed).at[sink].add(passed)
    items = jnp.searchsorted(jnp.cumsum(lengths), jnp.arange(rows * top), side="right").astype(jnp.int32)
    listing = items.reshape(top, rows).T
    listing = listing[jax.random.permutation(jax.random.fold_in(own, 1), rows)]
    rotation = jax.random.randint(jax.random.fold_in(own, 2), (rows, 1), 0, top)
    return jnp.take_along_axis(listing, (jnp.arange(top)[None, :] + rotation) % top, axis=1)


def portions_of(count, total, limit, skew, full):
    weights = [(1 << 20) // math.isqrt(grade ** skew) + 1 for grade in range(1, count + 1)]
    largest = limit if full else min(limit, max(-(-total // count), total * weights[0] // sum(weights)))
    least = 1 if total - largest >= count - 1 else 0
    holding, spare = [largest] + [least] * (count - 1), total - largest - least * (count - 1)
    while spare > 0:
        movable = [i for i in range(1, count) if holding[i] < largest] or [i for i in range(1, count) if holding[i] < limit]
        pool, remaining = sum([weights[i] for i in movable]), spare
        for i in movable:
            extra = min(limit - holding[i], max(1, remaining * weights[i] // pool), spare)
            holding[i] = holding[i] + extra
            spare = spare - extra
    return np.array(holding)


def normal_values(own_key, shape, scale, bound, split=(), kind=jnp.bfloat16):
    array = scale * jax.random.normal(own_key, shape, jnp.float32)
    if split:
        array = array * block_levels(own_key, shape, split, -0.22, 0.18)
    return jnp.clip(array, -bound, bound).astype(kind)


def setup_inputs(seed: int = 0, part: int = 0) -> dict:
    key_of = jax.random.split(jax.random.key(seed), 10)
    own_keys = jax.random.split(jax.random.fold_in(key_of[9], part), 10)
    template = normal_values(own_keys[0], (SUB_ROWS, N_PATCH * SUB_COLS), 1.0, 6.0, ((1, 16),), jnp.float32)
    science = normal_values(own_keys[1], (TOTAL_STRIPS, STRIP_ROWS, BLOCK), 1.0, 6.0, ((0, 16),), jnp.float32)
    dest_keys = jax.random.split(jax.random.fold_in(own_keys[2], 1), TOTAL_STRIPS // STRIPS)
    dest_turns = jax.random.permutation(jax.random.fold_in(own_keys[2], 3), TOTAL_STRIPS // STRIPS)
    dest = jax.vmap(lambda own, number: shared_out(jax.random.fold_in(own_keys[2], 2), own, number, STRIPS, N_PATCH, 1, CAP, 2))(dest_keys, dest_turns).reshape((TOTAL_STRIPS, 1))
    row_offset = plant(jax.random.randint(own_keys[3], (TOTAL_STRIPS,), 0, SUB_ROWS - STRIP_ROWS + 1), jax.random.fold_in(own_keys[3], 1), 0, SUB_ROWS - STRIP_ROWS).astype(jnp.int32)
    col_block = plant(jax.random.randint(own_keys[4], (TOTAL_STRIPS,), 0, SUB_COLS // BLOCK), jax.random.fold_in(own_keys[4], 1), 0, (SUB_COLS // BLOCK) - 1).astype(jnp.int32)
    basis_rows = normal_values(key_of[5], (BASES, TAPS), TAPS ** -0.5, 1.25, (), jnp.float32)
    basis_cols = normal_values(key_of[6], (BASES, TAPS), TAPS ** -0.5, 1.25, (), jnp.float32)
    stamp_rows = plant(jax.random.randint(own_keys[7], (N_PATCH, STAMPS), 0, SUB_ROWS), jax.random.fold_in(own_keys[7], 1), 0, SUB_ROWS - 1).astype(jnp.int32)
    stamp_cols = plant(jax.random.randint(own_keys[8], (N_PATCH, STAMPS), 0, SUB_COLS), jax.random.fold_in(own_keys[8], 1), 0, SUB_COLS - 1).astype(jnp.int32)
    return dict(template=template, science=science, dest=dest, row_offset=row_offset, col_block=col_block, basis_rows=basis_rows, basis_cols=basis_cols, stamp_rows=stamp_rows, stamp_cols=stamp_cols)


HIGH = lax.Precision.HIGHEST
RIDGE = 1.0

def filter_field(padded, row_taps, col_taps):
    taps = row_taps.shape[0]
    out_rows = padded.shape[0] - taps + 1
    out_cols = padded.shape[1] - taps + 1
    across = jnp.zeros((padded.shape[0], out_cols), jnp.float32)
    for shift_tap in range(taps):
        across = across + col_taps[shift_tap] * padded[:, shift_tap:shift_tap + out_cols]
    result = jnp.zeros((out_rows, out_cols), jnp.float32)
    for shift_tap in range(taps):
        result = result + row_taps[shift_tap] * across[shift_tap:shift_tap + out_rows, :]
    return result

def stamp_mask(row_start, blocks, stamp_r, stamp_c):
    rows_here = row_start[:, None] + jnp.arange(STRIP_ROWS, dtype=jnp.int32)[None, :]
    cols_here = blocks[:, None] * BLOCK + jnp.arange(BLOCK, dtype=jnp.int32)[None, :]
    row_hit = (jnp.abs(rows_here[:, :, None] - stamp_r[:, None, :]) <= STAMP_HALF).astype(jnp.float32)
    col_hit = (jnp.abs(stamp_c[:, :, None] - cols_here[:, None, :]) <= STAMP_HALF).astype(jnp.float32)
    counts = jnp.einsum('nis,nsj->nij', row_hit, col_hit, precision=HIGH)
    return jnp.minimum(counts, 1.0)

def cholesky_solve(matrix, rhs):
    factor = jnp.linalg.cholesky(matrix)
    inner = lax.linalg.triangular_solve(factor, rhs[..., None], left_side=True, lower=True)
    return lax.linalg.triangular_solve(factor, inner, left_side=True, lower=True, transpose_a=True)[..., 0]

def reference(template, science, dest, row_offset, col_block, basis_rows, basis_cols, stamp_rows, stamp_cols):
    half_taps = (TAPS - 1) // 2
    padded = jnp.pad(template, ((half_taps, half_taps), (half_taps, half_taps)))

    def one_basis(filters):
        return filter_field(padded, filters[0], filters[1])
    conv = lax.map(one_basis, (basis_rows, basis_cols))
    targets_all = dest[:, 0].astype(jnp.int32)

    def one_visit(visit):
        start = (visit * STRIPS).astype(jnp.int32)
        targets = lax.dynamic_slice_in_dim(targets_all, start, STRIPS)
        row_start = lax.dynamic_slice_in_dim(row_offset, start, STRIPS).astype(jnp.int32)
        blocks = lax.dynamic_slice_in_dim(col_block, start, STRIPS).astype(jnp.int32)
        pixels = lax.dynamic_slice_in_dim(science, start, STRIPS).reshape(STRIPS, -1)

        def window_of(target, first_row, block):
            return lax.dynamic_slice(conv, (jnp.int32(0), first_row, target * SUB_COLS + block * BLOCK), (BASES, STRIP_ROWS, BLOCK))
        windows = jax.vmap(window_of)(targets, row_start, blocks).reshape(STRIPS, BASES, -1)
        design = jnp.concatenate([windows, jnp.ones((STRIPS, 1, windows.shape[2]), jnp.float32)], axis=1)
        weight = stamp_mask(row_start, blocks, stamp_rows[targets], stamp_cols[targets]).reshape(STRIPS, 1, -1)
        weighted = design * weight
        normal = jnp.einsum('skp,slp->skl', weighted, design, precision=HIGH)
        moment = jnp.einsum('skp,sp->sk', weighted, pixels, precision=HIGH)
        owner_hot = (targets[:, None] == jnp.arange(N_PATCH, dtype=jnp.int32)[None, :]).astype(jnp.float32)
        columns = BASES + 1
        group_normal = jnp.einsum('sp,skl->pkl', owner_hot, normal, precision=HIGH) + RIDGE * jnp.eye(columns, dtype=jnp.float32)
        group_moment = jnp.einsum('sp,sk->pk', owner_hot, moment, precision=HIGH)
        coefficients = cholesky_solve(group_normal, group_moment)
        strip_coeff = jnp.einsum('sp,pk->sk', owner_hot, coefficients, precision=HIGH)
        model_image = jnp.einsum('skp,sk->sp', design, strip_coeff, precision=HIGH)
        return (pixels - model_image).reshape(STRIPS, STRIP_ROWS, BLOCK)
    result = lax.map(one_visit, jnp.arange(N_PATCH, dtype=jnp.int32))
    return result.reshape(N_PATCH * STRIPS, STRIP_ROWS, BLOCK)
```

```python
import functools
import math

import jax
import jax.numpy as jnp
from jax import lax
from jax.experimental import pallas as pl
from jax.experimental.pallas import tpu as pltpu
from jax.sharding import PartitionSpec as P

CAP = 2
STAMP_HALF = 10
RIDGE = 1.0
HIGH = lax.Precision.HIGHEST
F32 = jnp.float32
BF16 = jnp.bfloat16


def up(value, unit):
    return -(-value // unit) * unit


def split_in_two(values):
    high = values.astype(BF16)
    return high, (values - high.astype(F32)).astype(BF16)


def with_halo(cells, sides, width):
    for axis, dim in sides:
        count = lax.axis_size(axis)
        ends = count - 1
        head = lax.slice_in_dim(cells, 0, width, axis=dim)
        tail = lax.slice_in_dim(cells, cells.shape[dim] - width, cells.shape[dim], axis=dim)
        cells = jnp.concatenate(
            [
                lax.ppermute(tail, axis, [(i, (i + 1) % count) for i in range(ends)]),
                cells,
                lax.ppermute(head, axis, [((i + 1) % count, i) for i in range(ends)]),
            ],
            axis=dim,
        )
    return cells


def contract_last(left, right):
    return lax.dot_general(left, right, (((1,), (1,)), ((), ())), preferred_element_type=F32)


def fit_kernel(
    strip_rows,
    pos_ref,
    stamp_r_ref,
    stamp_c_ref,
    framed_ref,
    pixels_ref,
    rows_ref,
    cols_ref,
    out_ref,
    row_taps_ref,
    row_bands_ref,
    col_bands_ref,
    across_ref,
    design_ref,
    gram_ref,
):
    bases, taps = rows_ref.shape
    lanes = pixels_ref.shape[1]
    pair_rows = CAP * strip_rows
    n_rows = pixels_ref.shape[0]
    pairs = n_rows // pair_rows
    stamps = stamp_r_ref.shape[1]
    columns = bases + 1
    padded = up(columns + 1, 8)
    part = 2 * lanes // 4
    pitch = part // CAP
    step = pl.program_id(0)
    me = lax.axis_index("patch")

    @pl.when(step == 0)
    def _():
        sub = lax.broadcasted_iota(jnp.int32, (pair_rows, lanes), 0)
        wide_sub = lax.broadcasted_iota(jnp.int32, (lanes, lanes), 0)
        wide_lane = lax.broadcasted_iota(jnp.int32, (lanes, lanes), 1)
        row_taps_ref[...] = jnp.zeros_like(row_taps_ref)
        for k in range(bases):
            tap_row = jnp.concatenate(
                [rows_ref[k : k + 1, :], jnp.zeros((1, lanes - taps), F32)], axis=1
            )
            spread = pltpu.roll(
                jnp.broadcast_to(tap_row, (pair_rows, lanes)), 0, 1, stride=1, stride_axis=0
            )
            spread = jnp.where(sub < strip_rows, spread, pltpu.roll(spread, pitch - strip_rows, 1))
            row_taps_ref[pl.ds(k * pair_rows, pair_rows), :] = spread
            tap_col = jnp.concatenate(
                [cols_ref[k : k + 1, :], jnp.zeros((1, lanes - taps), F32)], axis=1
            )
            band = pltpu.roll(
                jnp.broadcast_to(tap_col, (lanes, lanes)), 0, 1, stride=1, stride_axis=0
            )
            for side in range(2):
                keep = wide_lane >= wide_sub if side == 0 else wide_lane < wide_sub
                high, low = split_in_two(jnp.where(keep, band, 0.0))
                col_bands_ref[k, 0:lanes, pl.ds(side * lanes, lanes)] = high
                col_bands_ref[k, lanes : 2 * lanes, pl.ds(side * lanes, lanes)] = low
        taps_f32 = row_taps_ref[...]
        taps_f32 = taps_f32 + pltpu.roll(taps_f32, part, 1)
        high, low = split_in_two(taps_f32)
        row_bands_ref[:, 0:lanes] = high
        row_bands_ref[:, lanes : 2 * lanes] = low

    for p in range(pairs):
        windows = []
        for c in range(CAP):
            slot = step * (pairs * CAP) + p * CAP + c
            first = pos_ref[slot, 0]
            block = pos_ref[slot, 1]
            over = lax.rem(first, 8)
            loaded = framed_ref[
                pl.ds(pl.multiple_of(first - over, 8), pitch + 8),
                pl.ds(pl.multiple_of(block * lanes, lanes), 2 * lanes),
            ]
            loaded = pltpu.roll(loaded, lax.rem(pitch + 8 - over, pitch + 8), 0)
            windows.append(loaded[:pitch])
        high, low = split_in_two(jnp.concatenate(windows, axis=0))
        stacked = jnp.concatenate([high, low, high, low], axis=0)
        across = jnp.dot(row_bands_ref[...], stacked, preferred_element_type=F32)
        for k in range(bases):
            across_ref[k, pl.ds(p * pair_rows, pair_rows), :] = across[
                k * pair_rows : (k + 1) * pair_rows, :
            ]

    for k in range(bases):
        high, low = split_in_two(across_ref[k])
        product = contract_last(jnp.concatenate([high, low], axis=0), col_bands_ref[k])
        product = product[:n_rows] + product[n_rows:]
        design_ref[pl.ds(k * n_rows, n_rows), :] = product[:, :lanes] + product[:, lanes:]
    design_ref[pl.ds(bases * n_rows, n_rows), :] = jnp.ones((n_rows, lanes), F32)
    design_ref[pl.ds(columns * n_rows, n_rows), :] = pixels_ref[...]
    for k in range(columns + 1, padded):
        design_ref[pl.ds(k * n_rows, n_rows), :] = jnp.zeros((n_rows, lanes), F32)

    sub = lax.broadcasted_iota(jnp.int32, (pair_rows, lanes), 0)
    lane = lax.broadcasted_iota(jnp.int32, (pair_rows, lanes), 1)
    for p in range(pairs):
        slot = step * (pairs * CAP) + p * CAP
        row_at = jnp.where(sub < strip_rows, pos_ref[slot, 0], pos_ref[slot + 1, 0] - strip_rows)
        col_at = jnp.where(sub < strip_rows, pos_ref[slot, 1], pos_ref[slot + 1, 1])
        live = jnp.where(sub < strip_rows, pos_ref[slot, 2], pos_ref[slot + 1, 2])
        row_at = (row_at + sub).astype(F32)
        col_at = (col_at * lanes + lane).astype(F32)
        nearest = jnp.full((pair_rows, lanes), 1e9, F32)
        for m in range(stamps):
            row_gap = jnp.abs(row_at - stamp_r_ref[me, m].astype(F32))
            col_gap = jnp.abs(col_at - stamp_c_ref[me, m].astype(F32))
            nearest = jnp.minimum(nearest, jnp.maximum(row_gap, col_gap))
        weight = jnp.where((nearest <= STAMP_HALF) & (live > 0), 1.0, 0.0)
        pieces = []
        for q in range(pair_rows):
            design = design_ref[pl.ds(p * pair_rows + q, padded, stride=n_rows), :]
            pieces.append(design * weight[q : q + 1, :])
        high, low = split_in_two(jnp.concatenate(pieces, axis=1))
        both = jnp.concatenate([high, low], axis=0)
        gram = contract_last(both, both)
        gram_ref[pl.ds(p * padded, padded), 0 : 2 * padded] = gram[:padded] + gram[padded:]

    tiles = padded // 8
    sub8 = lax.broadcasted_iota(jnp.int32, (8, pairs), 0)
    system = []
    for k in range(columns):
        turned = gram_ref[pl.ds(k, pairs, stride=padded), 0 : 2 * padded].T
        turned = turned[:padded] + turned[padded:]
        row = [turned[8 * t : 8 * t + 8] for t in range(tiles)]
        row[k // 8] = row[k // 8] + jnp.where(sub8 == k % 8, RIDGE, 0.0)
        system.append(row)
    for n in range(columns):
        at, within = n // 8, n % 8
        inverse = 1.0 / system[n][at][within : within + 1, :]
        pivot = [system[n][t] * inverse for t in range(at, tiles)]
        for k in range(columns):
            if k != n:
                factor = system[k][at][within : within + 1, :]
                for t in range(at, tiles):
                    system[k][t] = system[k][t] - factor * pivot[t - at]
        system[n][at:] = pivot
    at, within = columns // 8, columns % 8
    coeff = jnp.concatenate(
        [system[k][at][within : within + 1, :] for k in range(columns)]
        + [jnp.zeros((padded - columns, pairs), F32)],
        axis=0,
    ).T
    coeff = jnp.broadcast_to(coeff[:, None, :], (pairs, pair_rows, padded)).reshape(n_rows, padded)
    rest = pixels_ref[...]
    for k in range(columns):
        rest = rest - design_ref[pl.ds(k * n_rows, n_rows), :] * coeff[:, k : k + 1]
    out_ref[...] = rest


def fit(framed, pixels, positions, stamp_r, stamp_c, basis_rows, basis_cols, strip_rows):
    bases = basis_rows.shape[0]
    lanes = pixels.shape[1]
    slots = positions.shape[0]
    pair_rows = CAP * strip_rows
    pairs = math.gcd(slots // CAP, 16)
    n_rows = pairs * pair_rows
    padded = up(bases + 2, 8)
    even = up(bases, 2)
    smem = pl.BlockSpec(memory_space=pltpu.SMEM)
    whole = pl.BlockSpec(memory_space=pltpu.VMEM)
    block = pl.BlockSpec((n_rows, lanes), lambda i: (i, 0))
    return pl.pallas_call(
        functools.partial(fit_kernel, strip_rows),
        grid=(pixels.shape[0] // n_rows,),
        out_shape=jax.ShapeDtypeStruct(pixels.shape, F32),
        in_specs=[smem, smem, smem, whole, block, whole, whole],
        out_specs=block,
        scratch_shapes=[
            pltpu.VMEM((even * pair_rows, lanes), F32),
            pltpu.VMEM((even * pair_rows, 2 * lanes), BF16),
            pltpu.VMEM((bases, 2 * lanes, 2 * lanes), BF16),
            pltpu.VMEM((bases, n_rows, 2 * lanes), F32),
            pltpu.VMEM((padded * n_rows, lanes), F32),
            pltpu.VMEM((pairs * padded, lanes), F32),
        ],
        compiler_params=pltpu.CompilerParams(vmem_limit_bytes=48 << 20),
    )(positions, stamp_r, stamp_c, framed, pixels, basis_rows, basis_cols)


def on_device(
    template, science, dest, row_offset, col_block, basis_rows, basis_cols, stamp_rows, stamp_cols
):
    peers = lax.axis_size("patch")
    half_taps = (basis_rows.shape[1] - 1) // 2
    strips, strip_rows, block_cols = science.shape
    slots = peers * CAP
    haloed = with_halo(template, (("patch", 1),), half_taps)
    window = block_cols // 2 // CAP
    framed = jnp.pad(
        haloed,
        (
            (half_taps, window + 8 - strip_rows - half_taps),
            (0, block_cols - 2 * half_taps),
        ),
    )
    targets = dest[:, 0]
    strip_order = jnp.arange(strips, dtype=jnp.int32)
    earlier = (targets[:, None] == targets[None, :]) & (strip_order[None, :] < strip_order[:, None])
    rank_of = jnp.sum(earlier.astype(jnp.int32), axis=1)
    slot_of = targets * CAP + rank_of
    slot_ids = jnp.arange(slots, dtype=jnp.int32)
    slot_hot = (slot_ids[:, None] == slot_of[None, :]).astype(F32)
    strip_hot = (slot_of[:, None] == slot_ids[None, :]).astype(F32)
    positions = jnp.stack([row_offset, col_block, jnp.ones_like(row_offset)], axis=1).astype(F32)
    slot_info = jnp.dot(slot_hot, positions, precision=HIGH)
    outgoing = jnp.dot(slot_hot, science.reshape(strips, -1), precision=HIGH).reshape(
        slots, strip_rows, block_cols
    )
    arrived, arrived_info = (
        lax.all_to_all(outgoing, "patch", split_axis=0, concat_axis=0, tiled=True),
        lax.all_to_all(slot_info, "patch", split_axis=0, concat_axis=0, tiled=True),
    )
    residuals = fit(
        framed,
        arrived.reshape(slots * strip_rows, block_cols),
        arrived_info.astype(jnp.int32),
        stamp_rows,
        stamp_cols,
        basis_rows,
        basis_cols,
        strip_rows,
    ).reshape(slots, strip_rows, block_cols)
    returned = lax.all_to_all(residuals, "patch", split_axis=0, concat_axis=0, tiled=True)
    picked = jnp.dot(strip_hot, returned.reshape(slots, -1), precision=HIGH)
    return picked.reshape(strips, strip_rows, block_cols)


def solution(mesh):
    placed = (
        P(None, ("groups", "patch")),
        P(("groups", "patch"), None, None),
        P(("groups", "patch"), None),
        P(("groups", "patch")),
        P(("groups", "patch")),
        P(),
        P(),
        P("groups", None),
        P("groups", None),
    )
    return jax.shard_map(
        on_device,
        mesh=mesh,
        in_specs=placed,
        out_specs=P(("groups", "patch"), None, None),
        check_vma=False,
    )
```

```python
import math

import jax
import jax.numpy as jnp
from jax import lax
from jax.experimental import pallas as pl
from jax.experimental.pallas import tpu as pltpu
from jax.sharding import PartitionSpec as P

CAP = 2
STAMP_HALF = 10
RIDGE = 1.0
HIGH = lax.Precision.HIGHEST
MESH = pl.DeviceIdType.MESH
F32 = jnp.float32
BF16 = jnp.bfloat16


def up(value, unit):
    return -(-value // unit) * unit


def split_in_two(values):
    high = values.astype(BF16)
    return high, (values - high.astype(F32)).astype(BF16)


def contract_last(left, right):
    return lax.dot_general(left, right, (((1,), (1,)), ((), ())), preferred_element_type=F32)


def exact_dot(left, right):
    return jnp.dot(left, right, precision=HIGH, preferred_element_type=F32)


def iota(shape, dim):
    return lax.broadcasted_iota(jnp.int32, shape, dim)


def routes_of(dest_ref, peers):
    strips = dest_ref.shape[0]
    slots = peers * CAP
    square = (strips, strips)
    down, across = iota(square, 0), iota(square, 1)
    target_down = jnp.broadcast_to(dest_ref[...], square)
    target_across = jnp.sum(jnp.where(down == across, target_down, 0), axis=0, keepdims=True)
    same = jnp.where(target_down == target_across, 1, 0)
    rank_down = jnp.sum(jnp.where(across < down, same, 0), axis=1, keepdims=True)
    rank_across = jnp.sum(jnp.where(down < across, same, 0), axis=0, keepdims=True)
    slot_down = target_down[:, 0:1] * CAP + rank_down
    slot_across = target_across * CAP + rank_across
    return slot_down == iota((strips, slots), 1), slot_across == iota((slots, strips), 0)


def build_bands(rows_ref, cols_ref, row_taps_ref, row_bands_ref, col_bands_ref, strip_rows):
    bases, taps = rows_ref.shape
    lanes = row_taps_ref.shape[1]
    pair_rows = CAP * strip_rows
    part = 2 * lanes // 4
    pitch = part // CAP
    sub = iota((pair_rows, lanes), 0)
    keep = iota((lanes, lanes), 1) >= iota((lanes, lanes), 0)
    row_taps_ref[...] = jnp.zeros_like(row_taps_ref)
    blank = jnp.zeros((1, lanes - taps), F32)

    def one_basis(k, carry):
        tap_row = jnp.concatenate([rows_ref[pl.ds(k, 1), :], blank], axis=1)
        spread = pltpu.roll(
            jnp.broadcast_to(tap_row, (pair_rows, lanes)), 0, 1, stride=1, stride_axis=0
        )
        spread = jnp.where(sub < strip_rows, spread, pltpu.roll(spread, pitch - strip_rows, 1))
        row_taps_ref[pl.ds(pl.multiple_of(k * pair_rows, pair_rows), pair_rows), :] = spread
        tap_col = jnp.concatenate([cols_ref[pl.ds(k, 1), :], blank], axis=1)
        band = pltpu.roll(jnp.broadcast_to(tap_col, (lanes, lanes)), 0, 1, stride=1, stride_axis=0)
        for side in range(2):
            kept = jnp.where(keep, band, 0.0) if side == 0 else jnp.where(keep, 0.0, band)
            high, low = split_in_two(kept)
            col_bands_ref[k, 0:lanes, side * lanes : (side + 1) * lanes] = high
            col_bands_ref[k, lanes : 2 * lanes, side * lanes : (side + 1) * lanes] = low
        return carry

    lax.fori_loop(0, bases, one_basis, 0, unroll=bases)
    taps_f32 = row_taps_ref[...]
    taps_f32 = taps_f32 + pltpu.roll(taps_f32, part, 1)
    is_first = lax.rem(iota(taps_f32.shape, 0), pair_rows) < strip_rows
    for c in range(CAP):
        own = jnp.where(is_first, taps_f32, 0.0) if c == 0 else jnp.where(is_first, 0.0, taps_f32)
        for over in range(8):
            high, low = split_in_two(pltpu.roll(own, over, 1) if over else own)
            row_bands_ref[c, over, :, 0:lanes] = high
            row_bands_ref[c, over, :, lanes : 2 * lanes] = low


def fit_group(
    first_pair,
    pairs,
    strip_rows,
    top,
    bases,
    me,
    info_ref,
    stamp_r_ref,
    stamp_c_ref,
    framed_ref,
    pixels_ref,
    row_bands_ref,
    col_bands_ref,
    across_ref,
    design_ref,
    gram_ref,
    out_ref,
):
    lanes = pixels_ref.shape[1]
    pair_rows = CAP * strip_rows
    n_rows = pairs * pair_rows
    stamps = stamp_r_ref.shape[1]
    columns = bases + 1
    padded = up(columns + 1, 8)
    pitch = 2 * lanes // 4 // CAP
    group_rows = pl.ds(pl.multiple_of(first_pair * pair_rows, n_rows), n_rows)

    def filter_rows(p, carry):
        windows = []
        bands = None
        for c in range(CAP):
            at = (first_pair + p) * pair_rows + c * strip_rows
            first = info_ref[pl.ds(at, 1), :][0, 0] + top
            block = info_ref[pl.ds(at + 1, 1), :][0, 0]
            tile = lax.div(first, 8)
            sides = [
                framed_ref[block + side, pl.ds(tile, pitch // 8)].reshape(pitch, lanes)
                for side in range(2)
            ]
            windows.append(jnp.concatenate(sides, axis=1))
            own = row_bands_ref[c, lax.rem(first, 8)]
            bands = own if bands is None else bands + own
        high, low = split_in_two(jnp.concatenate(windows, axis=0))
        stacked = jnp.concatenate([high, low, high, low], axis=0)
        across = jnp.dot(bands, stacked, preferred_element_type=F32)
        across = across[: bases * pair_rows].reshape(bases, pair_rows, 2 * lanes)
        across_ref[:, pl.ds(pl.multiple_of(p * pair_rows, pair_rows), pair_rows), :] = across
        return carry

    lax.fori_loop(0, pairs, filter_rows, 0, unroll=pairs)

    def filter_cols(k, carry):
        high, low = split_in_two(across_ref[k])
        product = contract_last(jnp.concatenate([high, low], axis=0), col_bands_ref[k])
        product = product[:n_rows] + product[n_rows:]
        design_ref[pl.ds(pl.multiple_of(k * n_rows, n_rows), n_rows), :] = (
            product[:, :lanes] + product[:, lanes:]
        )
        return carry

    lax.fori_loop(0, bases, filter_cols, 0, unroll=bases)
    design_ref[bases * n_rows : columns * n_rows, :] = jnp.ones((n_rows, lanes), F32)
    design_ref[columns * n_rows : (columns + 1) * n_rows, :] = pixels_ref[group_rows, :]
    design_ref[(columns + 1) * n_rows :, :] = jnp.zeros(
        ((padded - columns - 1) * n_rows, lanes), F32
    )

    sub = iota((pair_rows, lanes), 0)
    lane = iota((pair_rows, lanes), 1)

    def normal_of(p, carry):
        tile = info_ref[
            pl.ds(pl.multiple_of((first_pair + p) * pair_rows, pair_rows), pair_rows), :
        ]

        def of_pair(item):
            return jnp.where(
                sub < strip_rows, tile[item : item + 1], tile[strip_rows + item : strip_rows + item + 1]
            )

        row_at = (of_pair(0) + lax.rem(sub, strip_rows)).astype(F32)
        col_at = (of_pair(1) * lanes + lane).astype(F32)
        nearest = jnp.full((pair_rows, lanes), 1e9, F32)
        for m in range(stamps):
            row_gap = jnp.abs(row_at - stamp_r_ref[me, m].astype(F32))
            col_gap = jnp.abs(col_at - stamp_c_ref[me, m].astype(F32))
            nearest = jnp.minimum(nearest, jnp.maximum(row_gap, col_gap))
        weight = jnp.where((nearest <= STAMP_HALF) & (of_pair(2) > 0), 1.0, 0.0)
        pieces = []
        for q in range(pair_rows):
            design = design_ref[pl.ds(p * pair_rows + q, padded, stride=n_rows), :]
            pieces.append(design * weight[q : q + 1, :])
        high, low = split_in_two(jnp.concatenate(pieces, axis=1))
        both = jnp.concatenate([high, low], axis=0)
        gram = contract_last(both, both)
        gram_ref[pl.ds(pl.multiple_of(p * padded, padded), padded), 0 : 2 * padded] = (
            gram[:padded] + gram[padded:]
        )
        return carry

    lax.fori_loop(0, pairs, normal_of, 0, unroll=pairs)

    unknown = iota((padded, pairs), 0)
    system = []
    for k in range(columns):
        turned = gram_ref[pl.ds(k, pairs, stride=padded), 0 : 2 * padded].T
        turned = turned[:padded] + turned[padded:]
        system.append(turned + jnp.where(unknown == k, RIDGE, 0.0))
    system = jnp.stack(system)
    for n in range(columns):
        within = n % 8
        if n and within == 0:
            system = system[:, 8:, :]
        pivot = system[n] * (1.0 / system[n, within : within + 1, :])
        rest = system - system[:, within : within + 1, :] * pivot[None]
        parts = [rest[:n], pivot[None], rest[n + 1 :]]
        system = jnp.concatenate([item for item in parts if item.shape[0]], axis=0)
    solved = columns - (columns - 1) // 8 * 8
    coeff = jnp.concatenate(
        [system[k, solved : solved + 1, :] for k in range(columns)]
        + [jnp.zeros((padded - columns, pairs), F32)],
        axis=0,
    ).T
    coeff = jnp.broadcast_to(coeff[:, None, :], (pairs, pair_rows, padded)).reshape(n_rows, padded)
    rest = pixels_ref[group_rows, :]
    for k in range(columns):
        rest = rest - design_ref[k * n_rows : (k + 1) * n_rows, :] * coeff[:, k : k + 1]
    out_ref[group_rows, :] = rest


def exchange(peers, me, pairs_of_refs, per_peer, sends, recvs):
    def rows_of(ref, peer):
        return ref.at[pl.ds(pl.multiple_of(peer * per_peer, per_peer), per_peer), :]

    def copies(offset, there, here):
        return [
            pltpu.make_async_remote_copy(
                src_ref=rows_of(source, there),
                dst_ref=rows_of(target, here),
                send_sem=sends.at[item, offset],
                recv_sem=recvs.at[item, offset],
                device_id={"patch": there},
                device_id_type=MESH,
            )
            for item, (source, target) in enumerate(pairs_of_refs)
        ]

    def start(offset, carry):
        for copy in copies(offset, lax.rem(me + offset, peers), me):
            copy.start()
        return carry

    def finish_recv(offset, carry):
        sender = lax.rem(me + peers - offset, peers)
        for copy in copies(offset, sender, sender):
            copy.wait_recv()
        return carry

    def finish_send(offset, carry):
        for copy in copies(offset, lax.rem(me + offset, peers), me):
            copy.wait_send()
        return carry

    def begin():
        lax.fori_loop(1, peers, start, 0)
        own = pl.ds(pl.multiple_of(me * per_peer, per_peer), per_peer)
        for source, target in pairs_of_refs:
            target[own, :] = source[own, :]

    return (
        begin,
        lambda: lax.fori_loop(1, peers, finish_recv, 0),
        lambda: lax.fori_loop(1, peers, finish_send, 0),
    )


def whole_kernel(
    template_ref,
    science_ref,
    dest_ref,
    offset_ref,
    block_ref,
    rows_ref,
    cols_ref,
    stamp_r_ref,
    stamp_c_ref,
    out_ref,
    row_taps_ref,
    row_bands_ref,
    col_bands_ref,
    across_ref,
    design_ref,
    gram_ref,
    framed_ref,
    left_ref,
    right_ref,
    send_pixels_ref,
    send_info_ref,
    pixels_ref,
    info_ref,
    residual_ref,
    returned_ref,
    go_sends,
    go_recvs,
    back_sends,
    back_recvs,
    halo_sends,
    halo_recvs,
):
    peers = lax.axis_size("patch")
    me = lax.axis_index("patch")
    strips, strip_rows, lanes = science_ref.shape
    sub_rows, sub_cols = template_ref.shape
    bases, taps = rows_ref.shape
    half = (taps - 1) // 2
    slots = peers * CAP
    pair_rows = CAP * strip_rows
    pairs = math.gcd(peers, 16)

    barrier = pltpu.get_barrier_semaphore()

    def greet(offset, carry):
        pl.semaphore_signal(
            barrier,
            inc=1,
            device_id={"patch": lax.rem(me + offset, peers)},
            device_id_type=MESH,
        )
        return carry

    lax.fori_loop(1, peers, greet, 0)

    strip_goes, slot_holds = routes_of(dest_ref, peers)
    strip_hot = jnp.where(strip_goes, 1.0, 0.0)
    slot_hot = jnp.where(slot_holds, 1.0, 0.0)
    for r in range(strip_rows):
        send_pixels_ref[pl.ds(r, slots, stride=strip_rows), :] = exact_dot(
            slot_hot, science_ref[:, r, :]
        )
    one = jnp.ones(offset_ref.shape, jnp.int32)
    for item, values in enumerate((offset_ref[...], block_ref[...], one)):
        chosen = jnp.sum(jnp.where(slot_holds, values, 0), axis=1, keepdims=True)
        send_info_ref[pl.ds(item, slots, stride=strip_rows), :] = jnp.broadcast_to(
            chosen, (slots, lanes)
        )
    send_info_ref[pl.ds(3, slots, stride=strip_rows), :] = jnp.zeros((slots, lanes), jnp.int32)

    go, go_recv, go_send = exchange(
        peers,
        me,
        ((send_info_ref, info_ref), (send_pixels_ref, pixels_ref)),
        pair_rows,
        go_sends,
        go_recvs,
    )
    back, back_recv, back_send = exchange(
        peers, me, ((residual_ref, returned_ref),), pair_rows, back_sends, back_recvs
    )
    halos = [
        pltpu.make_async_remote_copy(
            src_ref=template_ref.at[:, pl.ds(source, lanes)],
            dst_ref=target,
            send_sem=halo_sends.at[side],
            recv_sem=halo_recvs.at[side],
            device_id={"patch": lax.rem(me + move, peers)},
            device_id_type=MESH,
        )
        for side, (source, target, move) in enumerate(
            ((sub_cols - lanes, left_ref, 1), (0, right_ref, peers - 1))
        )
    ]

    pl.semaphore_wait(barrier, peers - 1)
    for copy in halos:
        copy.start()
    go()

    build_bands(rows_ref, cols_ref, row_taps_ref, row_bands_ref, col_bands_ref, strip_rows)
    top = up(half, 8)
    blocks, tiles = framed_ref.shape[:2]
    above, below = top // 8, (top + sub_rows) // 8
    framed_ref[:, 0:above] = jnp.zeros((blocks, above, 8, lanes), F32)
    framed_ref[:, below:] = jnp.zeros((blocks, tiles - below, 8, lanes), F32)
    for copy in halos:
        copy.wait_recv()
    left = jnp.where(me > 0, left_ref[...], 0.0)
    right = jnp.where(me < peers - 1, right_ref[...], 0.0)
    lane = iota((sub_rows, lanes), 1)
    wide = jnp.concatenate([template_ref[...], jnp.where(lane < half, right, 0.0)], axis=1)
    wide = pltpu.roll(wide, half, 1)
    first_block = jnp.where(lane < half, pltpu.roll(left, half, 1), wide[:, :lanes])
    for b in range(blocks):
        own = first_block if b == 0 else wide[:, b * lanes : (b + 1) * lanes]
        framed_ref[b, above:below] = own.reshape(below - above, 8, lanes)
    go_recv()

    def one_group(group):
        fit_group(
            group * pairs,
            pairs,
            strip_rows,
            top - half,
            bases,
            me,
            info_ref,
            stamp_r_ref,
            stamp_c_ref,
            framed_ref,
            pixels_ref,
            row_bands_ref,
            col_bands_ref,
            across_ref,
            design_ref,
            gram_ref,
            residual_ref,
        )

    if peers == pairs:
        one_group(0)
    else:
        pl.loop(0, peers // pairs)(one_group)

    back()
    back_recv()
    for r in range(strip_rows):
        out_ref[:, r, :] = exact_dot(
            strip_hot, returned_ref[pl.ds(r, slots, stride=strip_rows), :]
        )
    for copy in halos:
        copy.wait_send()
    go_send()
    back_send()


def on_device(
    template, science, dest, row_offset, col_block, basis_rows, basis_cols, stamp_rows, stamp_cols
):
    peers = lax.axis_size("patch")
    strips, strip_rows, lanes = science.shape
    sub_rows, sub_cols = template.shape
    bases, taps = basis_rows.shape
    pair_rows = CAP * strip_rows
    pairs = math.gcd(peers, 16)
    n_rows = pairs * pair_rows
    padded = up(bases + 2, 8)
    even = up(bases, 2)
    pitch = 2 * lanes // 4 // CAP
    half = (taps - 1) // 2
    tiles = (sub_rows - strip_rows + up(half, 8) - half) // 8 + pitch // 8
    smem = pl.BlockSpec(memory_space=pltpu.SMEM)
    vmem = pl.BlockSpec(memory_space=pltpu.VMEM)
    sems = pltpu.SemaphoreType.DMA
    return pl.pallas_call(
        whole_kernel,
        out_shape=jax.ShapeDtypeStruct(science.shape, F32),
        in_specs=[vmem] * 7 + [smem] * 2,
        out_specs=vmem,
        scratch_shapes=[
            pltpu.VMEM((even * pair_rows, lanes), F32),
            pltpu.VMEM((CAP, 8, even * pair_rows, 2 * lanes), BF16),
            pltpu.VMEM((bases, 2 * lanes, 2 * lanes), BF16),
            pltpu.VMEM((bases, n_rows, 2 * lanes), F32),
            pltpu.VMEM((padded * n_rows, lanes), F32),
            pltpu.VMEM((pairs * padded, lanes), F32),
            pltpu.VMEM((sub_cols // lanes + 1, tiles, 8, lanes), F32),
            pltpu.VMEM((sub_rows, lanes), F32),
            pltpu.VMEM((sub_rows, lanes), F32),
            pltpu.VMEM((peers * pair_rows, lanes), F32),
            pltpu.VMEM((peers * pair_rows, lanes), jnp.int32),
            pltpu.VMEM((peers * pair_rows, lanes), F32),
            pltpu.VMEM((peers * pair_rows, lanes), jnp.int32),
            pltpu.VMEM((peers * pair_rows, lanes), F32),
            pltpu.VMEM((peers * pair_rows, lanes), F32),
            sems((2, peers)),
            sems((2, peers)),
            sems((1, peers)),
            sems((1, peers)),
            sems((2,)),
            sems((2,)),
        ],
        compiler_params=pltpu.CompilerParams(
            collective_id=0, has_side_effects=True, vmem_limit_bytes=48 << 20
        ),
    )(
        template,
        science,
        dest,
        row_offset.reshape(1, strips),
        col_block.reshape(1, strips),
        basis_rows,
        basis_cols,
        stamp_rows,
        stamp_cols,
    )


def solution(mesh):
    placed = (
        P(None, ("groups", "patch")),
        P(("groups", "patch"), None, None),
        P(("groups", "patch"), None),
        P(("groups", "patch")),
        P(("groups", "patch")),
        P(),
        P(),
        P("groups", None),
        P("groups", None),
    )
    return jax.shard_map(
        on_device,
        mesh=mesh,
        in_specs=placed,
        out_specs=P(("groups", "patch"), None, None),
        check_vma=False,
    )
```

```python
import math

import jax
import jax.numpy as jnp
from jax import lax
from jax.experimental import pallas as pl
from jax.experimental.pallas import tpu as pltpu
from jax.sharding import PartitionSpec as P

CAP = 2
STAMP_HALF = 10
RIDGE = 1.0
HIGH = lax.Precision.HIGHEST
MESH = pl.DeviceIdType.MESH
ITEMS = 3
NOWHERE = -(1 << 20)
F32 = jnp.float32
BF16 = jnp.bfloat16


def up(value, unit):
    return -(-value // unit) * unit


def split_in_two(values):
    high = values.astype(BF16)
    return high, (values - high.astype(F32)).astype(BF16)


def contract_last(left, right):
    return lax.dot_general(left, right, (((1,), (1,)), ((), ())), preferred_element_type=F32)


def exact_dot(left, right):
    return jnp.dot(left, right, precision=HIGH, preferred_element_type=F32)


def iota(shape, dim):
    return lax.broadcasted_iota(jnp.int32, shape, dim)


def routes_of(targets, peers):
    strips = targets.shape[1]
    square = (strips, strips)
    down, across = iota(square, 0), iota(square, 1)
    target_across = jnp.broadcast_to(targets, square)
    target_down = jnp.sum(jnp.where(down == across, target_across, 0), axis=1, keepdims=True)
    same = jnp.where(target_down == target_across, 1, 0)
    rank_down = jnp.sum(jnp.where(across < down, same, 0), axis=1, keepdims=True)
    rank_across = jnp.sum(jnp.where(down < across, same, 0), axis=0, keepdims=True)
    return target_down * CAP + rank_down, targets * CAP + rank_across


def build_bands(row_basis, col_basis, row_taps_ref, row_bands_ref, col_bands_ref, strip_rows):
    bases, taps = row_basis.shape
    lanes = row_taps_ref.shape[1]
    pair_rows = CAP * strip_rows
    part = 2 * lanes // 4
    pitch = part // CAP
    sub = iota((pair_rows, lanes), 0)
    keep = iota((lanes, lanes), 1) >= iota((lanes, lanes), 0)
    row_taps_ref[...] = jnp.zeros_like(row_taps_ref)
    blank = jnp.zeros((1, lanes - taps), F32)

    for k in range(bases):
        tap_row = jnp.concatenate([row_basis[k : k + 1, :], blank], axis=1)
        spread = pltpu.roll(
            jnp.broadcast_to(tap_row, (pair_rows, lanes)), 0, 1, stride=1, stride_axis=0
        )
        spread = jnp.where(sub < strip_rows, spread, pltpu.roll(spread, pitch - strip_rows, 1))
        row_taps_ref[k * pair_rows : (k + 1) * pair_rows, :] = spread
        tap_col = jnp.concatenate([col_basis[k : k + 1, :], blank], axis=1)
        band = pltpu.roll(jnp.broadcast_to(tap_col, (lanes, lanes)), 0, 1, stride=1, stride_axis=0)
        for side in range(2):
            kept = jnp.where(keep, band, 0.0) if side == 0 else jnp.where(keep, 0.0, band)
            high, low = split_in_two(kept)
            col_bands_ref[k, 0:lanes, side * lanes : (side + 1) * lanes] = high
            col_bands_ref[k, lanes : 2 * lanes, side * lanes : (side + 1) * lanes] = low
    taps_f32 = row_taps_ref[...]
    taps_f32 = taps_f32 + pltpu.roll(taps_f32, part, 1)
    is_first = lax.rem(iota(taps_f32.shape, 0), pair_rows) < strip_rows
    for c in range(CAP):
        own = jnp.where(is_first, taps_f32, 0.0) if c == 0 else jnp.where(is_first, 0.0, taps_f32)
        for over in range(8):
            high, low = split_in_two(pltpu.roll(own, over, 1) if over else own)
            row_bands_ref[c, over, :, 0:lanes] = high
            row_bands_ref[c, over, :, lanes : 2 * lanes] = low


def fit_group(
    first_pair,
    pairs,
    strip_rows,
    top,
    bases,
    me,
    info_ref,
    stamp_r_ref,
    stamp_c_ref,
    framed_ref,
    pixels_ref,
    row_bands_ref,
    col_bands_ref,
    across_ref,
    design_ref,
    gram_ref,
    out_ref,
    await_pixels,
):
    lanes = pixels_ref.shape[1]
    pair_rows = CAP * strip_rows
    n_rows = pairs * pair_rows
    stamps = stamp_r_ref.shape[1]
    columns = bases + 1
    padded = up(columns + 1, 8)
    pitch = 2 * lanes // 4 // CAP
    group_rows = pl.ds(pl.multiple_of(first_pair * pair_rows, n_rows), n_rows)

    def filter_rows(p, carry):
        windows = []
        bands = None
        for c in range(CAP):
            info = info_ref[first_pair + p]
            first = info[0, ITEMS * c] + top
            block = info[0, ITEMS * c + 1]
            tile = lax.div(first, 8)
            sides = [
                framed_ref[block + side, pl.ds(tile, pitch // 8)].reshape(pitch, lanes)
                for side in range(2)
            ]
            windows.append(jnp.concatenate(sides, axis=1))
            own = row_bands_ref[c, lax.rem(first, 8)]
            bands = own if bands is None else bands + own
        high, low = split_in_two(jnp.concatenate(windows, axis=0))
        stacked = jnp.concatenate([high, low, high, low], axis=0)
        across = jnp.dot(bands, stacked, preferred_element_type=F32)
        across = across[: bases * pair_rows].reshape(bases, pair_rows, 2 * lanes)
        across_ref[:, pl.ds(pl.multiple_of(p * pair_rows, pair_rows), pair_rows), :] = across
        return carry

    lax.fori_loop(0, pairs, filter_rows, 0, unroll=pairs)

    def filter_cols(k, carry):
        high, low = split_in_two(across_ref[k])
        product = contract_last(jnp.concatenate([high, low], axis=0), col_bands_ref[k])
        product = product[:n_rows] + product[n_rows:]
        design_ref[pl.ds(pl.multiple_of(k * n_rows, n_rows), n_rows), :] = (
            product[:, :lanes] + product[:, lanes:]
        )
        return carry

    lax.fori_loop(0, bases, filter_cols, 0, unroll=bases)
    await_pixels()
    design_ref[bases * n_rows : columns * n_rows, :] = jnp.ones((n_rows, lanes), F32)
    design_ref[columns * n_rows : (columns + 1) * n_rows, :] = pixels_ref[group_rows, :]
    design_ref[(columns + 1) * n_rows :, :] = jnp.zeros(
        ((padded - columns - 1) * n_rows, lanes), F32
    )

    sub = iota((pair_rows, lanes), 0)
    lane = iota((pair_rows, lanes), 1)

    def normal_of(p, carry):
        info = info_ref[first_pair + p]

        def of_pair(item):
            return jnp.where(sub < strip_rows, info[0, item], info[0, ITEMS + item])

        row_at = (of_pair(2) + lax.rem(sub, strip_rows)).astype(F32)
        col_at = (of_pair(1) * lanes + lane).astype(F32)
        nearest = jnp.full((pair_rows, lanes), 1e9, F32)
        for m in range(stamps):
            row_gap = jnp.abs(row_at - stamp_r_ref[me, m].astype(F32))
            col_gap = jnp.abs(col_at - stamp_c_ref[me, m].astype(F32))
            nearest = jnp.minimum(nearest, jnp.maximum(row_gap, col_gap))
        weight = jnp.where(nearest <= STAMP_HALF, 1.0, 0.0)
        pieces = []
        for q in range(pair_rows):
            design = design_ref[pl.ds(p * pair_rows + q, padded, stride=n_rows), :]
            pieces.append(design * weight[q : q + 1, :])
        high, low = split_in_two(jnp.concatenate(pieces, axis=1))
        both = jnp.concatenate([high, low], axis=0)
        gram = contract_last(both, both)
        gram_ref[pl.ds(pl.multiple_of(p * padded, padded), padded), 0 : 2 * padded] = (
            gram[:padded] + gram[padded:]
        )
        return carry

    lax.fori_loop(0, pairs, normal_of, 0, unroll=pairs)

    unknown = iota((padded, pairs), 0)
    system = []
    for k in range(columns):
        turned = gram_ref[pl.ds(k, pairs, stride=padded), 0 : 2 * padded].T
        turned = turned[:padded] + turned[padded:]
        system.append(turned + jnp.where(unknown == k, RIDGE, 0.0))
    system = jnp.stack(system)
    for n in range(columns):
        within = n % 8
        if n and within == 0:
            system = system[:, 8:, :]
        pivot = system[n] * (1.0 / system[n, within : within + 1, :])
        rest = system - system[:, within : within + 1, :] * pivot[None]
        parts = [rest[:n], pivot[None], rest[n + 1 :]]
        system = jnp.concatenate([item for item in parts if item.shape[0]], axis=0)
    solved = columns - (columns - 1) // 8 * 8
    coeff = jnp.concatenate(
        [system[k, solved : solved + 1, :] for k in range(columns)]
        + [jnp.zeros((padded - columns, pairs), F32)],
        axis=0,
    ).T
    coeff = jnp.broadcast_to(coeff[:, None, :], (pairs, pair_rows, padded)).reshape(n_rows, padded)
    rest = pixels_ref[group_rows, :]
    for k in range(columns):
        rest = rest - design_ref[k * n_rows : (k + 1) * n_rows, :] * coeff[:, k : k + 1]
    out_ref[group_rows, :] = rest


def exchange(peers, me, pairs_of_refs, per_peer, sends, recvs):
    def rows_of(ref, peer):
        if len(ref.shape) == 3:
            return ref.at[peer]
        return ref.at[pl.ds(pl.multiple_of(peer * per_peer, per_peer), per_peer), :]

    def copies(offset, there, here):
        return [
            pltpu.make_async_remote_copy(
                src_ref=rows_of(source, there),
                dst_ref=rows_of(target, here),
                send_sem=sends.at[item, offset],
                recv_sem=recvs.at[item, offset],
                device_id={"patch": there},
                device_id_type=MESH,
            )
            for item, (source, target) in enumerate(pairs_of_refs)
        ]

    def start(offset, carry):
        for copy in copies(offset, lax.rem(me + offset, peers), me):
            copy.start()
        return carry

    def finish_recv(offset, carry):
        sender = lax.rem(me + peers - offset, peers)
        for copy in copies(offset, sender, sender):
            copy.wait_recv()
        return carry

    def finish_send(offset, carry):
        for copy in copies(offset, lax.rem(me + offset, peers), me):
            copy.wait_send()
        return carry

    def begin():
        lax.fori_loop(1, peers, start, 0)
        own = pl.ds(pl.multiple_of(me * per_peer, per_peer), per_peer)
        for source, target in pairs_of_refs:
            if len(source.shape) == 3:
                target[me] = source[me]
            else:
                target[own, :] = source[own, :]

    return (
        begin,
        lambda: lax.fori_loop(1, peers, finish_recv, 0),
        lambda: lax.fori_loop(1, peers, finish_send, 0),
    )


def whole_kernel(
    template_hbm,
    science_hbm,
    dest_hbm,
    offset_hbm,
    block_hbm,
    rows_hbm,
    cols_hbm,
    stamp_r_hbm,
    stamp_c_hbm,
    out_ref,
    template_ref,
    science_ref,
    dest_ref,
    offset_ref,
    block_ref,
    rows_ref,
    cols_ref,
    stamp_r_ref,
    stamp_c_ref,
    row_taps_ref,
    row_bands_ref,
    col_bands_ref,
    across_ref,
    design_ref,
    gram_ref,
    framed_ref,
    left_ref,
    right_ref,
    send_pixels_ref,
    send_info_ref,
    pixels_ref,
    info_ref,
    residual_ref,
    returned_ref,
    info_sends,
    info_recvs,
    go_sends,
    go_recvs,
    back_sends,
    back_recvs,
    halo_sends,
    halo_recvs,
    fetched,
):
    peers = lax.axis_size("patch")
    me = lax.axis_index("patch")
    strips, strip_rows, lanes = science_ref.shape
    sub_rows, sub_cols = template_ref.shape
    taps, bases = rows_ref.shape
    half = (taps - 1) // 2
    slots = peers * CAP
    pair_rows = CAP * strip_rows
    pairs = math.gcd(peers, 16)

    barrier = pltpu.get_barrier_semaphore()

    def greet(offset, carry):
        pl.semaphore_signal(
            barrier,
            inc=1,
            device_id={"patch": lax.rem(me + offset, peers)},
            device_id_type=MESH,
        )
        return carry

    lax.fori_loop(1, peers, greet, 0)
    fetches = [
        pltpu.make_async_copy(source, target, fetched.at[item])
        for item, (source, target) in enumerate(
            (
                (dest_hbm, dest_ref),
                (offset_hbm, offset_ref),
                (block_hbm, block_ref),
                (science_hbm, science_ref),
                (template_hbm, template_ref),
                (rows_hbm, rows_ref),
                (cols_hbm, cols_ref),
                (stamp_r_hbm, stamp_r_ref),
                (stamp_c_hbm, stamp_c_ref),
            )
        )
    ]
    for fetch in fetches:
        fetch.start()
    top = up(half, 8)
    blocks, tiles = framed_ref.shape[:2]
    above, below = top // 8, (top + sub_rows) // 8
    framed_ref[:, 0:above] = jnp.zeros((blocks, above, 8, lanes), F32)
    framed_ref[:, below:] = jnp.zeros((blocks, tiles - below, 8, lanes), F32)
    for fetch in fetches[:4]:
        fetch.wait()

    slot_down, slot_across = routes_of(dest_ref[...], peers)
    info_lane = iota((peers, lanes), 1)
    info = jnp.zeros((peers, lanes), jnp.int32)
    for c in range(CAP):
        holds = slot_across == iota((peers, strips), 0) * CAP + c
        for item, (values, empty) in enumerate(
            ((offset_ref[...], 0), (block_ref[...], 0), (offset_ref[...], NOWHERE))
        ):
            chosen = empty + jnp.sum(
                jnp.where(holds, values - empty, 0), axis=1, keepdims=True
            )
            info = jnp.where(info_lane == ITEMS * c + item, chosen, info)
    send_info_ref[:, 0, :] = info
    tell, tell_recv, tell_send = exchange(
        peers, me, ((send_info_ref, info_ref),), pair_rows, info_sends, info_recvs
    )
    go, go_recv, go_send = exchange(
        peers, me, ((send_pixels_ref, pixels_ref),), pair_rows, go_sends, go_recvs
    )
    back, back_recv, back_send = exchange(
        peers, me, ((residual_ref, returned_ref),), pair_rows, back_sends, back_recvs
    )
    halos = [
        pltpu.make_async_remote_copy(
            src_ref=template_ref.at[:, pl.ds(source, lanes)],
            dst_ref=target,
            send_sem=halo_sends.at[side],
            recv_sem=halo_recvs.at[side],
            device_id={"patch": lax.rem(me + move, peers)},
            device_id_type=MESH,
        )
        for side, (source, target, move) in enumerate(
            ((sub_cols - lanes, left_ref, 1), (0, right_ref, peers - 1))
        )
    ]

    slot_hot = jnp.where(slot_across == iota((slots, strips), 0), 1.0, 0.0)
    for r in range(strip_rows):
        send_pixels_ref[pl.ds(r, slots, stride=strip_rows), :] = exact_dot(
            slot_hot, science_ref[:, r, :]
        )
    fetches[4].wait()
    pl.semaphore_wait(barrier, peers - 1)
    tell()

    @pl.when(me < peers - 1)
    def _():
        halos[0].start()

    @pl.when(me > 0)
    def _():
        halos[1].start()

    go()

    for fetch in fetches[5:]:
        fetch.wait()
    build_bands(
        rows_ref[...].T, cols_ref[...].T, row_taps_ref, row_bands_ref, col_bands_ref, strip_rows
    )
    @pl.when(me > 0)
    def _():
        halos[0].wait_recv()

    @pl.when(me < peers - 1)
    def _():
        halos[1].wait_recv()

    left = jnp.where(me > 0, left_ref[...], 0.0)
    right = jnp.where(me < peers - 1, right_ref[...], 0.0)
    lane = iota((sub_rows, lanes), 1)
    wide = jnp.concatenate([template_ref[...], jnp.where(lane < half, right, 0.0)], axis=1)
    wide = pltpu.roll(wide, half, 1)
    first_block = jnp.where(lane < half, pltpu.roll(left, half, 1), wide[:, :lanes])
    for b in range(blocks):
        own = first_block if b == 0 else wide[:, b * lanes : (b + 1) * lanes]
        framed_ref[b, above:below] = own.reshape(below - above, 8, lanes)
    tell_recv()
    if peers != pairs:
        go_recv()

    def one_group(group):
        fit_group(
            group * pairs,
            pairs,
            strip_rows,
            top - half,
            bases,
            me,
            info_ref,
            stamp_r_ref,
            stamp_c_ref,
            framed_ref,
            pixels_ref,
            row_bands_ref,
            col_bands_ref,
            across_ref,
            design_ref,
            gram_ref,
            residual_ref,
            go_recv if peers == pairs else lambda: None,
        )

    if peers == pairs:
        one_group(0)
    else:
        pl.loop(0, peers // pairs)(one_group)

    back()
    back_recv()
    strip_hot = jnp.where(slot_down == iota((strips, slots), 1), 1.0, 0.0)
    for r in range(strip_rows):
        out_ref[:, r, :] = exact_dot(
            strip_hot, returned_ref[pl.ds(r, slots, stride=strip_rows), :]
        )

    @pl.when(me < peers - 1)
    def _():
        halos[0].wait_send()

    @pl.when(me > 0)
    def _():
        halos[1].wait_send()

    tell_send()
    go_send()
    back_send()


def on_device(
    template, science, dest, row_offset, col_block, basis_rows, basis_cols, stamp_rows, stamp_cols
):
    peers = lax.axis_size("patch")
    strips, strip_rows, lanes = science.shape
    sub_rows, sub_cols = template.shape
    bases, taps = basis_rows.shape
    pair_rows = CAP * strip_rows
    pairs = math.gcd(peers, 16)
    n_rows = pairs * pair_rows
    padded = up(bases + 2, 8)
    even = up(bases, 2)
    pitch = 2 * lanes // 4 // CAP
    half = (taps - 1) // 2
    tiles = (sub_rows - strip_rows + up(half, 8) - half) // 8 + pitch // 8
    vmem = pl.BlockSpec(memory_space=pltpu.VMEM)
    sems = pltpu.SemaphoreType.DMA
    return pl.pallas_call(
        whole_kernel,
        out_shape=jax.ShapeDtypeStruct(science.shape, F32),
        in_specs=[pl.BlockSpec(memory_space=pltpu.HBM)] * 9,
        out_specs=vmem,
        scratch_shapes=[
            pltpu.VMEM(template.shape, F32),
            pltpu.VMEM(science.shape, F32),
            pltpu.VMEM((1, strips), jnp.int32),
            pltpu.VMEM((1, strips), jnp.int32),
            pltpu.VMEM((1, strips), jnp.int32),
            pltpu.VMEM((taps, bases), F32),
            pltpu.VMEM((taps, bases), F32),
            pltpu.SMEM(stamp_rows.shape, jnp.int32),
            pltpu.SMEM(stamp_cols.shape, jnp.int32),
            pltpu.VMEM((even * pair_rows, lanes), F32),
            pltpu.VMEM((CAP, 8, even * pair_rows, 2 * lanes), BF16),
            pltpu.VMEM((bases, 2 * lanes, 2 * lanes), BF16),
            pltpu.VMEM((bases, n_rows, 2 * lanes), F32),
            pltpu.VMEM((padded * n_rows, lanes), F32),
            pltpu.VMEM((pairs * padded, lanes), F32),
            pltpu.VMEM((sub_cols // lanes + 1, tiles, 8, lanes), F32),
            pltpu.VMEM((sub_rows, lanes), F32),
            pltpu.VMEM((sub_rows, lanes), F32),
            pltpu.VMEM((peers * pair_rows, lanes), F32),
            pltpu.VMEM((peers, 1, lanes), jnp.int32),
            pltpu.VMEM((peers * pair_rows, lanes), F32),
            pltpu.VMEM((peers, 1, lanes), jnp.int32),
            pltpu.VMEM((peers * pair_rows, lanes), F32),
            pltpu.VMEM((peers * pair_rows, lanes), F32),
            sems((1, peers)),
            sems((1, peers)),
            sems((1, peers)),
            sems((1, peers)),
            sems((1, peers)),
            sems((1, peers)),
            sems((2,)),
            sems((2,)),
            sems((9,)),
        ],
        compiler_params=pltpu.CompilerParams(
            collective_id=0, has_side_effects=True, vmem_limit_bytes=62 << 20
        ),
    )(
        template,
        science,
        dest.reshape(1, strips),
        row_offset.reshape(1, strips),
        col_block.reshape(1, strips),
        basis_rows.T,
        basis_cols.T,
        stamp_rows,
        stamp_cols,
    )


def solution(mesh):
    placed = (
        P(None, ("groups", "patch")),
        P(("groups", "patch"), None, None),
        P(("groups", "patch"), None),
        P(("groups", "patch")),
        P(("groups", "patch")),
        P(),
        P(),
        P("groups", None),
        P("groups", None),
    )
    return jax.shard_map(
        on_device,
        mesh=mesh,
        in_specs=placed,
        out_specs=P(("groups", "patch"), None, None),
        check_vma=False,
    )
```

```python
import math

import jax
import jax.numpy as jnp
from jax import lax
from jax.experimental import pallas as pl
from jax.experimental.pallas import tpu as pltpu
from jax.sharding import PartitionSpec as P

CAP = 2
STAMP_HALF = 10
RIDGE = 1.0
HIGH = lax.Precision.HIGHEST
MESH = pl.DeviceIdType.MESH
ITEMS = 3
NOWHERE = -(1 << 20)
F32 = jnp.float32
BF16 = jnp.bfloat16


def up(value, unit):
    return -(-value // unit) * unit


def split_in_two(values):
    high = values.astype(BF16)
    return high, (values - high.astype(F32)).astype(BF16)


def contract_last(left, right):
    return lax.dot_general(left, right, (((1,), (1,)), ((), ())), preferred_element_type=F32)


def exact_dot(left, right):
    return jnp.dot(left, right, precision=HIGH, preferred_element_type=F32)


def iota(shape, dim):
    return lax.broadcasted_iota(jnp.int32, shape, dim)


def routes_of(targets, peers):
    strips = targets.shape[1]
    square = (strips, strips)
    down, across = iota(square, 0), iota(square, 1)
    target_across = jnp.broadcast_to(targets, square)
    target_down = jnp.sum(jnp.where(down == across, target_across, 0), axis=1, keepdims=True)
    same = jnp.where(target_down == target_across, 1, 0)
    rank_down = jnp.sum(jnp.where(across < down, same, 0), axis=1, keepdims=True)
    rank_across = jnp.sum(jnp.where(down < across, same, 0), axis=0, keepdims=True)
    return target_down * CAP + rank_down, targets * CAP + rank_across


def build_bands(row_basis, col_basis, row_taps_ref, row_bands_ref, col_bands_ref, strip_rows):
    bases, taps = row_basis.shape
    lanes = row_taps_ref.shape[1]
    pair_rows = CAP * strip_rows
    part = 2 * lanes // 4
    pitch = part // CAP
    sub = iota((pair_rows, lanes), 0)
    keep = iota((lanes, lanes), 1) >= iota((lanes, lanes), 0)
    row_taps_ref[...] = jnp.zeros_like(row_taps_ref)
    blank = jnp.zeros((1, lanes - taps), F32)

    for k in range(bases):
        tap_row = jnp.concatenate([row_basis[k : k + 1, :], blank], axis=1)
        spread = pltpu.roll(
            jnp.broadcast_to(tap_row, (pair_rows, lanes)), 0, 1, stride=1, stride_axis=0
        )
        spread = jnp.where(sub < strip_rows, spread, pltpu.roll(spread, pitch - strip_rows, 1))
        row_taps_ref[k * pair_rows : (k + 1) * pair_rows, :] = spread
        tap_col = jnp.concatenate([col_basis[k : k + 1, :], blank], axis=1)
        band = pltpu.roll(jnp.broadcast_to(tap_col, (lanes, lanes)), 0, 1, stride=1, stride_axis=0)
        for side in range(2):
            kept = jnp.where(keep, band, 0.0) if side == 0 else jnp.where(keep, 0.0, band)
            high, low = split_in_two(kept)
            col_bands_ref[k, 0:lanes, side * lanes : (side + 1) * lanes] = high
            col_bands_ref[k, lanes : 2 * lanes, side * lanes : (side + 1) * lanes] = low
    taps_f32 = row_taps_ref[...]
    taps_f32 = taps_f32 + pltpu.roll(taps_f32, part, 1)
    is_first = lax.rem(iota(taps_f32.shape, 0), pair_rows) < strip_rows
    for c in range(CAP):
        own = jnp.where(is_first, taps_f32, 0.0) if c == 0 else jnp.where(is_first, 0.0, taps_f32)
        for over in range(8):
            high, low = split_in_two(pltpu.roll(own, over, 1) if over else own)
            row_bands_ref[c, over, :, 0:lanes] = high
            row_bands_ref[c, over, :, lanes : 2 * lanes] = low


def fit_group(
    first_pair,
    pairs,
    strip_rows,
    top,
    bases,
    me,
    info_ref,
    stamp_r_ref,
    stamp_c_ref,
    framed_ref,
    pixels_ref,
    row_bands_ref,
    col_bands_ref,
    across_ref,
    weight_ref,
    design_ref,
    gram_ref,
    out_ref,
    await_pixels,
):
    lanes = pixels_ref.shape[1]
    pair_rows = CAP * strip_rows
    n_rows = pairs * pair_rows
    stamps = stamp_r_ref.shape[1]
    columns = bases + 1
    padded = up(columns + 1, 8)
    pitch = 2 * lanes // 4 // CAP
    group_rows = pl.ds(pl.multiple_of(first_pair * pair_rows, n_rows), n_rows)

    sub = iota((pair_rows, lanes), 0)
    lane = iota((pair_rows, lanes), 1)
    is_first = sub < strip_rows
    centres = [
        (stamp_r_ref[me, m].astype(F32), stamp_c_ref[me, m].astype(F32)) for m in range(stamps)
    ]

    def filter_rows(p, carry):
        windows = []
        bands = None
        info = info_ref[first_pair + p]
        for c in range(CAP):
            first = info[0, ITEMS * c] + top
            block = info[0, ITEMS * c + 1]
            tile = lax.div(first, 8)
            sides = [
                framed_ref[block + side, pl.ds(tile, pitch // 8)].reshape(pitch, lanes)
                for side in range(2)
            ]
            windows.append(jnp.concatenate(sides, axis=1))
            own = row_bands_ref[c, lax.rem(first, 8)]
            bands = own if bands is None else bands + own
        high, low = split_in_two(jnp.concatenate(windows, axis=0))
        stacked = jnp.concatenate([high, low, high, low], axis=0)
        across = jnp.dot(bands, stacked, preferred_element_type=F32)
        across = across[: bases * pair_rows].reshape(bases, pair_rows, 2 * lanes)
        rows_here = pl.ds(pl.multiple_of(p * pair_rows, pair_rows), pair_rows)
        across_ref[:, rows_here, :] = across

        def of_pair(item):
            return jnp.where(is_first, info[0, item], info[0, ITEMS + item])

        row_at = (of_pair(2) + lax.rem(sub, strip_rows)).astype(F32)
        col_at = (of_pair(1) * lanes + lane).astype(F32)
        nearest = jnp.full((pair_rows, lanes), 1e9, F32)
        for centre_r, centre_c in centres:
            gap = jnp.maximum(jnp.abs(row_at - centre_r), jnp.abs(col_at - centre_c))
            nearest = jnp.minimum(nearest, gap)
        weight_ref[rows_here, :] = jnp.where(nearest <= STAMP_HALF, 1.0, 0.0)
        return carry

    lax.fori_loop(0, pairs, filter_rows, 0, unroll=pairs)

    def filter_cols(k, carry):
        high, low = split_in_two(across_ref[k])
        product = contract_last(jnp.concatenate([high, low], axis=0), col_bands_ref[k])
        product = product[:n_rows] + product[n_rows:]
        design_ref[pl.ds(pl.multiple_of(k * n_rows, n_rows), n_rows), :] = (
            product[:, :lanes] + product[:, lanes:]
        )
        return carry

    lax.fori_loop(0, bases, filter_cols, 0, unroll=bases)
    await_pixels()
    design_ref[bases * n_rows : columns * n_rows, :] = jnp.ones((n_rows, lanes), F32)
    design_ref[columns * n_rows : (columns + 1) * n_rows, :] = pixels_ref[group_rows, :]
    design_ref[(columns + 1) * n_rows :, :] = jnp.zeros(
        ((padded - columns - 1) * n_rows, lanes), F32
    )

    def normal_of(p, carry):
        pieces = []
        for q in range(pair_rows):
            design = design_ref[pl.ds(p * pair_rows + q, padded, stride=n_rows), :]
            pieces.append(design * weight_ref[pl.ds(p * pair_rows + q, 1), :])
        high, low = split_in_two(jnp.concatenate(pieces, axis=1))
        both = jnp.concatenate([high, low], axis=0)
        gram = contract_last(both, both)
        gram_ref[pl.ds(pl.multiple_of(p * padded, padded), padded), 0 : 2 * padded] = (
            gram[:padded] + gram[padded:]
        )
        return carry

    lax.fori_loop(0, pairs, normal_of, 0, unroll=pairs)

    unknown = iota((padded, pairs), 0)
    system = []
    for k in range(columns):
        turned = gram_ref[pl.ds(k, pairs, stride=padded), 0 : 2 * padded].T
        turned = turned[:padded] + turned[padded:]
        system.append(turned + jnp.where(unknown == k, RIDGE, 0.0))
    system = jnp.stack(system)
    for n in range(columns):
        within = n % 8
        if n and within == 0:
            system = system[:, 8:, :]
        pivot = system[n] * (1.0 / system[n, within : within + 1, :])
        rest = system - system[:, within : within + 1, :] * pivot[None]
        parts = [rest[:n], pivot[None], rest[n + 1 :]]
        system = jnp.concatenate([item for item in parts if item.shape[0]], axis=0)
    solved = columns - (columns - 1) // 8 * 8
    coeff = jnp.concatenate(
        [system[k, solved : solved + 1, :] for k in range(columns)]
        + [jnp.zeros((padded - columns, pairs), F32)],
        axis=0,
    ).T
    coeff = jnp.broadcast_to(coeff[:, None, :], (pairs, pair_rows, padded)).reshape(n_rows, padded)
    rest = pixels_ref[group_rows, :]
    for k in range(columns):
        rest = rest - design_ref[k * n_rows : (k + 1) * n_rows, :] * coeff[:, k : k + 1]
    out_ref[group_rows, :] = rest


def exchange(peers, me, pairs_of_refs, per_peer, sends, recvs):
    def rows_of(ref, peer):
        if len(ref.shape) == 3:
            return ref.at[peer]
        return ref.at[pl.ds(pl.multiple_of(peer * per_peer, per_peer), per_peer), :]

    def copies(offset, there, here):
        return [
            pltpu.make_async_remote_copy(
                src_ref=rows_of(source, there),
                dst_ref=rows_of(target, here),
                send_sem=sends.at[item, offset],
                recv_sem=recvs.at[item, offset],
                device_id={"patch": there},
                device_id_type=MESH,
            )
            for item, (source, target) in enumerate(pairs_of_refs)
        ]

    def start(offset, carry):
        for copy in copies(offset, lax.rem(me + offset, peers), me):
            copy.start()
        return carry

    def finish_recv(offset, carry):
        sender = lax.rem(me + peers - offset, peers)
        for copy in copies(offset, sender, sender):
            copy.wait_recv()
        return carry

    def finish_send(offset, carry):
        for copy in copies(offset, lax.rem(me + offset, peers), me):
            copy.wait_send()
        return carry

    def begin():
        lax.fori_loop(1, peers, start, 0)
        own = pl.ds(pl.multiple_of(me * per_peer, per_peer), per_peer)
        for source, target in pairs_of_refs:
            if len(source.shape) == 3:
                target[me] = source[me]
            else:
                target[own, :] = source[own, :]

    return (
        begin,
        lambda: lax.fori_loop(1, peers, finish_recv, 0),
        lambda: lax.fori_loop(1, peers, finish_send, 0),
    )


def whole_kernel(
    template_hbm,
    science_hbm,
    dest_hbm,
    offset_hbm,
    block_hbm,
    rows_hbm,
    cols_hbm,
    stamp_r_hbm,
    stamp_c_hbm,
    out_ref,
    template_ref,
    science_ref,
    dest_ref,
    offset_ref,
    block_ref,
    rows_ref,
    cols_ref,
    stamp_r_ref,
    stamp_c_ref,
    row_taps_ref,
    row_bands_ref,
    col_bands_ref,
    across_ref,
    weight_ref,
    design_ref,
    gram_ref,
    framed_ref,
    left_ref,
    right_ref,
    send_pixels_ref,
    send_info_ref,
    pixels_ref,
    info_ref,
    residual_ref,
    returned_ref,
    info_sends,
    info_recvs,
    go_sends,
    go_recvs,
    back_sends,
    back_recvs,
    halo_sends,
    halo_recvs,
    fetched,
):
    peers = lax.axis_size("patch")
    me = lax.axis_index("patch")
    strips, strip_rows, lanes = science_ref.shape
    sub_rows, sub_cols = template_ref.shape
    taps, bases = rows_ref.shape
    half = (taps - 1) // 2
    slots = peers * CAP
    pair_rows = CAP * strip_rows
    pairs = math.gcd(peers, 16)

    barrier = pltpu.get_barrier_semaphore()

    def greet(offset, carry):
        pl.semaphore_signal(
            barrier,
            inc=1,
            device_id={"patch": lax.rem(me + offset, peers)},
            device_id_type=MESH,
        )
        return carry

    lax.fori_loop(1, peers, greet, 0)
    fetches = [
        pltpu.make_async_copy(source, target, fetched.at[item])
        for item, (source, target) in enumerate(
            (
                (dest_hbm, dest_ref),
                (offset_hbm, offset_ref),
                (block_hbm, block_ref),
                (science_hbm, science_ref),
                (template_hbm, template_ref),
                (rows_hbm, rows_ref),
                (cols_hbm, cols_ref),
                (stamp_r_hbm, stamp_r_ref),
                (stamp_c_hbm, stamp_c_ref),
            )
        )
    ]
    for fetch in fetches:
        fetch.start()
    top = up(half, 8)
    blocks, tiles = framed_ref.shape[:2]
    above, below = top // 8, (top + sub_rows) // 8
    framed_ref[:, 0:above] = jnp.zeros((blocks, above, 8, lanes), F32)
    framed_ref[:, below:] = jnp.zeros((blocks, tiles - below, 8, lanes), F32)
    for fetch in fetches[:4]:
        fetch.wait()

    slot_down, slot_across = routes_of(dest_ref[...], peers)
    info_lane = iota((peers, lanes), 1)
    info = jnp.zeros((peers, lanes), jnp.int32)
    for c in range(CAP):
        holds = slot_across == iota((peers, strips), 0) * CAP + c
        for item, (values, empty) in enumerate(
            ((offset_ref[...], 0), (block_ref[...], 0), (offset_ref[...], NOWHERE))
        ):
            chosen = empty + jnp.sum(
                jnp.where(holds, values - empty, 0), axis=1, keepdims=True
            )
            info = jnp.where(info_lane == ITEMS * c + item, chosen, info)
    send_info_ref[:, 0, :] = info
    tell, tell_recv, tell_send = exchange(
        peers, me, ((send_info_ref, info_ref),), pair_rows, info_sends, info_recvs
    )
    go, go_recv, go_send = exchange(
        peers, me, ((send_pixels_ref, pixels_ref),), pair_rows, go_sends, go_recvs
    )
    back, back_recv, back_send = exchange(
        peers, me, ((residual_ref, returned_ref),), pair_rows, back_sends, back_recvs
    )
    halos = [
        pltpu.make_async_remote_copy(
            src_ref=template_ref.at[:, pl.ds(source, lanes)],
            dst_ref=target,
            send_sem=halo_sends.at[side],
            recv_sem=halo_recvs.at[side],
            device_id={"patch": lax.rem(me + move, peers)},
            device_id_type=MESH,
        )
        for side, (source, target, move) in enumerate(
            ((sub_cols - lanes, left_ref, 1), (0, right_ref, peers - 1))
        )
    ]

    slot_hot = jnp.where(slot_across == iota((slots, strips), 0), 1.0, 0.0)
    for r in range(strip_rows):
        send_pixels_ref[pl.ds(r, slots, stride=strip_rows), :] = exact_dot(
            slot_hot, science_ref[:, r, :]
        )
    fetches[4].wait()
    pl.semaphore_wait(barrier, peers - 1)
    tell()

    @pl.when(me < peers - 1)
    def _():
        halos[0].start()

    @pl.when(me > 0)
    def _():
        halos[1].start()

    go()

    for fetch in fetches[5:]:
        fetch.wait()
    build_bands(
        rows_ref[...].T, cols_ref[...].T, row_taps_ref, row_bands_ref, col_bands_ref, strip_rows
    )
    @pl.when(me > 0)
    def _():
        halos[0].wait_recv()

    @pl.when(me < peers - 1)
    def _():
        halos[1].wait_recv()

    left = jnp.where(me > 0, left_ref[...], 0.0)
    right = jnp.where(me < peers - 1, right_ref[...], 0.0)
    lane = iota((sub_rows, lanes), 1)
    wide = jnp.concatenate([template_ref[...], jnp.where(lane < half, right, 0.0)], axis=1)
    wide = pltpu.roll(wide, half, 1)
    first_block = jnp.where(lane < half, pltpu.roll(left, half, 1), wide[:, :lanes])
    for b in range(blocks):
        own = first_block if b == 0 else wide[:, b * lanes : (b + 1) * lanes]
        framed_ref[b, above:below] = own.reshape(below - above, 8, lanes)
    tell_recv()
    if peers != pairs:
        go_recv()

    def one_group(group):
        fit_group(
            group * pairs,
            pairs,
            strip_rows,
            top - half,
            bases,
            me,
            info_ref,
            stamp_r_ref,
            stamp_c_ref,
            framed_ref,
            pixels_ref,
            row_bands_ref,
            col_bands_ref,
            across_ref,
            weight_ref,
            design_ref,
            gram_ref,
            residual_ref,
            go_recv if peers == pairs else lambda: None,
        )

    if peers == pairs:
        one_group(0)
    else:
        pl.loop(0, peers // pairs)(one_group)

    back()
    back_recv()
    strip_hot = jnp.where(slot_down == iota((strips, slots), 1), 1.0, 0.0)
    for r in range(strip_rows):
        out_ref[:, r, :] = exact_dot(
            strip_hot, returned_ref[pl.ds(r, slots, stride=strip_rows), :]
        )

    @pl.when(me < peers - 1)
    def _():
        halos[0].wait_send()

    @pl.when(me > 0)
    def _():
        halos[1].wait_send()

    tell_send()
    go_send()
    back_send()


def on_device(
    template, science, dest, row_offset, col_block, basis_rows, basis_cols, stamp_rows, stamp_cols
):
    peers = lax.axis_size("patch")
    strips, strip_rows, lanes = science.shape
    sub_rows, sub_cols = template.shape
    bases, taps = basis_rows.shape
    pair_rows = CAP * strip_rows
    pairs = math.gcd(peers, 16)
    n_rows = pairs * pair_rows
    padded = up(bases + 2, 8)
    even = up(bases, 2)
    pitch = 2 * lanes // 4 // CAP
    half = (taps - 1) // 2
    tiles = (sub_rows - strip_rows + up(half, 8) - half) // 8 + pitch // 8
    vmem = pl.BlockSpec(memory_space=pltpu.VMEM)
    sems = pltpu.SemaphoreType.DMA
    return pl.pallas_call(
        whole_kernel,
        out_shape=jax.ShapeDtypeStruct(science.shape, F32),
        in_specs=[pl.BlockSpec(memory_space=pltpu.HBM)] * 9,
        out_specs=vmem,
        scratch_shapes=[
            pltpu.VMEM(template.shape, F32),
            pltpu.VMEM(science.shape, F32),
            pltpu.VMEM((1, strips), jnp.int32),
            pltpu.VMEM((1, strips), jnp.int32),
            pltpu.VMEM((1, strips), jnp.int32),
            pltpu.VMEM((taps, bases), F32),
            pltpu.VMEM((taps, bases), F32),
            pltpu.SMEM(stamp_rows.shape, jnp.int32),
            pltpu.SMEM(stamp_cols.shape, jnp.int32),
            pltpu.VMEM((even * pair_rows, lanes), F32),
            pltpu.VMEM((CAP, 8, even * pair_rows, 2 * lanes), BF16),
            pltpu.VMEM((bases, 2 * lanes, 2 * lanes), BF16),
            pltpu.VMEM((bases, n_rows, 2 * lanes), F32),
            pltpu.VMEM((n_rows, lanes), F32),
            pltpu.VMEM((padded * n_rows, lanes), F32),
            pltpu.VMEM((pairs * padded, lanes), F32),
            pltpu.VMEM((sub_cols // lanes + 1, tiles, 8, lanes), F32),
            pltpu.VMEM((sub_rows, lanes), F32),
            pltpu.VMEM((sub_rows, lanes), F32),
            pltpu.VMEM((peers * pair_rows, lanes), F32),
            pltpu.VMEM((peers, 1, lanes), jnp.int32),
            pltpu.VMEM((peers * pair_rows, lanes), F32),
            pltpu.VMEM((peers, 1, lanes), jnp.int32),
            pltpu.VMEM((peers * pair_rows, lanes), F32),
            pltpu.VMEM((peers * pair_rows, lanes), F32),
            sems((1, peers)),
            sems((1, peers)),
            sems((1, peers)),
            sems((1, peers)),
            sems((1, peers)),
            sems((1, peers)),
            sems((2,)),
            sems((2,)),
            sems((9,)),
        ],
        compiler_params=pltpu.CompilerParams(
            collective_id=0, has_side_effects=True, vmem_limit_bytes=48 << 20
        ),
    )(
        template,
        science,
        dest.reshape(1, strips),
        row_offset.reshape(1, strips),
        col_block.reshape(1, strips),
        basis_rows.T,
        basis_cols.T,
        stamp_rows,
        stamp_cols,
    )


def solution(mesh):
    placed = (
        P(None, ("groups", "patch")),
        P(("groups", "patch"), None, None),
        P(("groups", "patch"), None),
        P(("groups", "patch")),
        P(("groups", "patch")),
        P(),
        P(),
        P("groups", None),
        P("groups", None),
    )
    return jax.shard_map(
        on_device,
        mesh=mesh,
        in_specs=placed,
        out_specs=P(("groups", "patch"), None, None),
        check_vma=False,
    )
```

```python
import math

import jax
import jax.numpy as jnp
from jax import lax
from jax.experimental import pallas as pl
from jax.experimental.pallas import tpu as pltpu
from jax.sharding import PartitionSpec as P

CAP = 2
STAMP_HALF = 10
RIDGE = 1.0
HIGH = lax.Precision.HIGHEST
MESH = pl.DeviceIdType.MESH
ITEMS = 3
NOWHERE = -(1 << 20)
F32 = jnp.float32
BF16 = jnp.bfloat16


def up(value, unit):
    return -(-value // unit) * unit


def split_in_two(values):
    high = values.astype(BF16)
    return high, (values - high.astype(F32)).astype(BF16)


def contract_last(left, right):
    return lax.dot_general(left, right, (((1,), (1,)), ((), ())), preferred_element_type=F32)


def exact_dot(left, right):
    return jnp.dot(left, right, precision=HIGH, preferred_element_type=F32)


def iota(shape, dim):
    return lax.broadcasted_iota(jnp.int32, shape, dim)


def routes_of(targets, peers):
    strips = targets.shape[1]
    square = (strips, strips)
    down, across = iota(square, 0), iota(square, 1)
    target_across = jnp.broadcast_to(targets, square)
    target_down = jnp.sum(jnp.where(down == across, target_across, 0), axis=1, keepdims=True)
    same = jnp.where(target_down == target_across, 1, 0)
    rank_down = jnp.sum(jnp.where(across < down, same, 0), axis=1, keepdims=True)
    rank_across = jnp.sum(jnp.where(down < across, same, 0), axis=0, keepdims=True)
    return target_down * CAP + rank_down, targets * CAP + rank_across


def build_bands(row_basis, col_basis, row_taps_ref, row_bands_ref, col_bands_ref, strip_rows):
    bases, taps = row_basis.shape
    lanes = row_taps_ref.shape[1]
    pair_rows = CAP * strip_rows
    part = 2 * lanes // 4
    pitch = part // CAP
    sub = iota((pair_rows, lanes), 0)
    keep = iota((lanes, lanes), 1) >= iota((lanes, lanes), 0)
    row_taps_ref[...] = jnp.zeros_like(row_taps_ref)
    blank = jnp.zeros((1, lanes - taps), F32)

    for k in range(bases):
        tap_row = jnp.concatenate([row_basis[k : k + 1, :], blank], axis=1)
        spread = pltpu.roll(
            jnp.broadcast_to(tap_row, (pair_rows, lanes)), 0, 1, stride=1, stride_axis=0
        )
        spread = jnp.where(sub < strip_rows, spread, pltpu.roll(spread, pitch - strip_rows, 1))
        row_taps_ref[k * pair_rows : (k + 1) * pair_rows, :] = spread
        tap_col = jnp.concatenate([col_basis[k : k + 1, :], blank], axis=1)
        band = pltpu.roll(jnp.broadcast_to(tap_col, (lanes, lanes)), 0, 1, stride=1, stride_axis=0)
        for side in range(2):
            kept = jnp.where(keep, band, 0.0) if side == 0 else jnp.where(keep, 0.0, band)
            high, low = split_in_two(kept)
            col_bands_ref[k, 0:lanes, side * lanes : (side + 1) * lanes] = high
            col_bands_ref[k, lanes : 2 * lanes, side * lanes : (side + 1) * lanes] = low
    taps_f32 = row_taps_ref[...]
    taps_f32 = taps_f32 + pltpu.roll(taps_f32, part, 1)
    is_first = lax.rem(iota(taps_f32.shape, 0), pair_rows) < strip_rows
    for c in range(CAP):
        own = jnp.where(is_first, taps_f32, 0.0) if c == 0 else jnp.where(is_first, 0.0, taps_f32)
        for over in range(8):
            high, low = split_in_two(pltpu.roll(own, over, 1) if over else own)
            row_bands_ref[c, over, :, 0:lanes] = high
            row_bands_ref[c, over, :, lanes : 2 * lanes] = low


def fit_group(
    first_pair,
    pairs,
    strip_rows,
    top,
    bases,
    me,
    info_ref,
    stamp_r_ref,
    stamp_c_ref,
    framed_ref,
    pixels_ref,
    row_bands_ref,
    col_bands_ref,
    across_ref,
    weight_ref,
    design_ref,
    gram_ref,
    out_ref,
    await_pixels,
):
    lanes = pixels_ref.shape[1]
    pair_rows = CAP * strip_rows
    n_rows = pairs * pair_rows
    stamps = stamp_r_ref.shape[1]
    columns = bases + 1
    padded = up(columns + 1, 8)
    pitch = 2 * lanes // 4 // CAP
    group_rows = pl.ds(pl.multiple_of(first_pair * pair_rows, n_rows), n_rows)

    sub = iota((pair_rows, lanes), 0)
    lane = iota((pair_rows, lanes), 1)
    is_first = sub < strip_rows
    centres = [
        (stamp_r_ref[me, m].astype(F32), stamp_c_ref[me, m].astype(F32)) for m in range(stamps)
    ]

    def filter_rows(p, carry):
        windows = []
        bands = None
        info = info_ref[first_pair + p]
        for c in range(CAP):
            first = info[0, ITEMS * c] + top
            block = info[0, ITEMS * c + 1]
            tile = lax.div(first, 8)
            sides = [
                framed_ref[block + side, pl.ds(tile, pitch // 8)].reshape(pitch, lanes)
                for side in range(2)
            ]
            windows.append(jnp.concatenate(sides, axis=1))
            own = row_bands_ref[c, lax.rem(first, 8)]
            bands = own if bands is None else bands + own
        high, low = split_in_two(jnp.concatenate(windows, axis=0))
        stacked = jnp.concatenate([high, low, high, low], axis=0)
        across = jnp.dot(bands, stacked, preferred_element_type=F32)
        across = across[: bases * pair_rows].reshape(bases, pair_rows, 2 * lanes)
        rows_here = pl.ds(pl.multiple_of(p * pair_rows, pair_rows), pair_rows)
        across_ref[:, rows_here, :] = across

        def of_pair(item):
            return jnp.where(is_first, info[0, item], info[0, ITEMS + item])

        row_at = (of_pair(2) + lax.rem(sub, strip_rows)).astype(F32)
        col_at = (of_pair(1) * lanes + lane).astype(F32)
        nearest = jnp.full((pair_rows, lanes), 1e9, F32)
        for centre_r, centre_c in centres:
            gap = jnp.maximum(jnp.abs(row_at - centre_r), jnp.abs(col_at - centre_c))
            nearest = jnp.minimum(nearest, gap)
        weight_ref[rows_here, :] = jnp.where(nearest <= STAMP_HALF, 1.0, 0.0)
        return carry

    lax.fori_loop(0, pairs, filter_rows, 0, unroll=pairs)

    def filter_cols(k, carry):
        high, low = split_in_two(across_ref[k])
        product = contract_last(jnp.concatenate([high, low], axis=0), col_bands_ref[k])
        product = product[:n_rows] + product[n_rows:]
        design_ref[pl.ds(pl.multiple_of(k * n_rows, n_rows), n_rows), :] = (
            product[:, :lanes] + product[:, lanes:]
        )
        return carry

    lax.fori_loop(0, bases, filter_cols, 0, unroll=bases)
    await_pixels()
    design_ref[bases * n_rows : columns * n_rows, :] = jnp.ones((n_rows, lanes), F32)
    design_ref[columns * n_rows : (columns + 1) * n_rows, :] = pixels_ref[group_rows, :]
    design_ref[(columns + 1) * n_rows :, :] = jnp.zeros(
        ((padded - columns - 1) * n_rows, lanes), F32
    )

    def normal_of(p, carry):
        pieces = []
        for q in range(pair_rows):
            design = design_ref[pl.ds(p * pair_rows + q, padded, stride=n_rows), :]
            pieces.append(design * weight_ref[pl.ds(p * pair_rows + q, 1), :])
        high, low = split_in_two(jnp.concatenate(pieces, axis=1))
        both = jnp.concatenate([high, low], axis=0)
        gram = contract_last(both, both)
        gram_ref[pl.ds(pl.multiple_of(p * padded, padded), padded), 0 : 2 * padded] = (
            gram[:padded] + gram[padded:]
        )
        return carry

    lax.fori_loop(0, pairs, normal_of, 0, unroll=pairs)

    unknown = iota((padded, pairs), 0)
    system = []
    for k in range(columns):
        turned = gram_ref[pl.ds(k, pairs, stride=padded), 0 : 2 * padded].T
        turned = turned[:padded] + turned[padded:]
        system.append(turned + jnp.where(unknown == k, RIDGE, 0.0))
    system = jnp.stack(system)
    for n in range(columns):
        within = n % 8
        if n and within == 0:
            system = system[:, 8:, :]
        pivot = system[n] * (1.0 / system[n, within : within + 1, :])
        rest = system - system[:, within : within + 1, :] * pivot[None]
        parts = [rest[:n], pivot[None], rest[n + 1 :]]
        system = jnp.concatenate([item for item in parts if item.shape[0]], axis=0)
    solved = columns - (columns - 1) // 8 * 8
    coeff = jnp.concatenate(
        [system[k, solved : solved + 1, :] for k in range(columns)]
        + [jnp.zeros((padded - columns, pairs), F32)],
        axis=0,
    ).T
    coeff = jnp.broadcast_to(coeff[:, None, :], (pairs, pair_rows, padded)).reshape(n_rows, padded)
    rest = pixels_ref[group_rows, :]
    for k in range(columns):
        rest = rest - design_ref[k * n_rows : (k + 1) * n_rows, :] * coeff[:, k : k + 1]
    out_ref[group_rows, :] = rest


def exchange(peers, me, pairs_of_refs, per_peer, sends, recvs):
    def rows_of(ref, peer):
        if len(ref.shape) == 3:
            return ref.at[peer]
        return ref.at[pl.ds(pl.multiple_of(peer * per_peer, per_peer), per_peer), :]

    def copies(offset, there, here):
        return [
            pltpu.make_async_remote_copy(
                src_ref=rows_of(source, there),
                dst_ref=rows_of(target, here),
                send_sem=sends.at[item, offset],
                recv_sem=recvs.at[item, offset],
                device_id={"patch": there},
                device_id_type=MESH,
            )
            for item, (source, target) in enumerate(pairs_of_refs)
        ]

    def start(offset, carry):
        for copy in copies(offset, lax.rem(me + offset, peers), me):
            copy.start()
        return carry

    def finish_recv(offset, carry):
        sender = lax.rem(me + peers - offset, peers)
        for copy in copies(offset, sender, sender):
            copy.wait_recv()
        return carry

    def finish_send(offset, carry):
        for copy in copies(offset, lax.rem(me + offset, peers), me):
            copy.wait_send()
        return carry

    def begin():
        lax.fori_loop(1, peers, start, 0)
        own = pl.ds(pl.multiple_of(me * per_peer, per_peer), per_peer)
        for source, target in pairs_of_refs:
            if len(source.shape) == 3:
                target[me] = source[me]
            else:
                target[own, :] = source[own, :]

    return (
        begin,
        lambda: lax.fori_loop(1, peers, finish_recv, 0),
        lambda: lax.fori_loop(1, peers, finish_send, 0),
    )


def whole_kernel(
    template_hbm,
    science_hbm,
    dest_hbm,
    offset_hbm,
    block_hbm,
    rows_hbm,
    cols_hbm,
    stamp_r_hbm,
    stamp_c_hbm,
    out_ref,
    template_ref,
    science_ref,
    dest_ref,
    offset_ref,
    block_ref,
    rows_ref,
    cols_ref,
    stamp_r_ref,
    stamp_c_ref,
    row_taps_ref,
    row_bands_ref,
    col_bands_ref,
    across_ref,
    weight_ref,
    design_ref,
    gram_ref,
    framed_ref,
    left_ref,
    right_ref,
    send_pixels_ref,
    send_info_ref,
    pixels_ref,
    info_ref,
    residual_ref,
    returned_ref,
    info_sends,
    info_recvs,
    go_sends,
    go_recvs,
    back_sends,
    back_recvs,
    halo_sends,
    halo_recvs,
    fetched,
):
    peers = lax.axis_size("patch")
    me = lax.axis_index("patch")
    strips, strip_rows, lanes = science_ref.shape
    sub_rows, sub_cols = template_ref.shape
    taps, bases = rows_ref.shape
    half = (taps - 1) // 2
    slots = peers * CAP
    pair_rows = CAP * strip_rows
    pairs = math.gcd(peers, 16)

    barrier = pltpu.get_barrier_semaphore()

    def greet(offset, carry):
        pl.semaphore_signal(
            barrier,
            inc=1,
            device_id={"patch": lax.rem(me + offset, peers)},
            device_id_type=MESH,
        )
        return carry

    lax.fori_loop(1, peers, greet, 0)
    fetches = [
        pltpu.make_async_copy(source, target, fetched.at[item])
        for item, (source, target) in enumerate(
            (
                (dest_hbm, dest_ref),
                (offset_hbm, offset_ref),
                (block_hbm, block_ref),
                (science_hbm, science_ref),
                (template_hbm, template_ref),
                (rows_hbm, rows_ref),
                (cols_hbm, cols_ref),
                (stamp_r_hbm, stamp_r_ref),
                (stamp_c_hbm, stamp_c_ref),
            )
        )
    ]
    for fetch in fetches:
        fetch.start()
    top = up(half, 8)
    blocks, tiles = framed_ref.shape[:2]
    above, below = top // 8, (top + sub_rows) // 8
    framed_ref[:, 0:above] = jnp.zeros((blocks, above, 8, lanes), F32)
    framed_ref[:, below:] = jnp.zeros((blocks, tiles - below, 8, lanes), F32)
    for fetch in fetches[:3]:
        fetch.wait()

    slot_down, slot_across = routes_of(dest_ref[...], peers)
    info_lane = iota((peers, lanes), 1)
    info = jnp.zeros((peers, lanes), jnp.int32)
    for c in range(CAP):
        holds = slot_across == iota((peers, strips), 0) * CAP + c
        for item, (values, empty) in enumerate(
            ((offset_ref[...], 0), (block_ref[...], 0), (offset_ref[...], NOWHERE))
        ):
            chosen = empty + jnp.sum(
                jnp.where(holds, values - empty, 0), axis=1, keepdims=True
            )
            info = jnp.where(info_lane == ITEMS * c + item, chosen, info)
    send_info_ref[:, 0, :] = info
    tell, tell_recv, tell_send = exchange(
        peers, me, ((send_info_ref, info_ref),), pair_rows, info_sends, info_recvs
    )
    go, go_recv, go_send = exchange(
        peers, me, ((send_pixels_ref, pixels_ref),), pair_rows, go_sends, go_recvs
    )
    back, back_recv, back_send = exchange(
        peers, me, ((residual_ref, returned_ref),), pair_rows, back_sends, back_recvs
    )
    halos = [
        pltpu.make_async_remote_copy(
            src_ref=template_ref.at[:, pl.ds(source, lanes)],
            dst_ref=target,
            send_sem=halo_sends.at[side],
            recv_sem=halo_recvs.at[side],
            device_id={"patch": lax.rem(me + move, peers)},
            device_id_type=MESH,
        )
        for side, (source, target, move) in enumerate(
            ((sub_cols - lanes, left_ref, 1), (0, right_ref, peers - 1))
        )
    ]

    fetches[4].wait()
    pl.semaphore_wait(barrier, peers - 1)
    tell()

    @pl.when(me < peers - 1)
    def _():
        halos[0].start()

    @pl.when(me > 0)
    def _():
        halos[1].start()

    fetches[3].wait()
    slot_hot = jnp.where(slot_across == iota((slots, strips), 0), 1.0, 0.0)
    for r in range(strip_rows):
        send_pixels_ref[pl.ds(r, slots, stride=strip_rows), :] = exact_dot(
            slot_hot, science_ref[:, r, :]
        )
    go()

    for fetch in fetches[5:]:
        fetch.wait()
    build_bands(
        rows_ref[...].T, cols_ref[...].T, row_taps_ref, row_bands_ref, col_bands_ref, strip_rows
    )
    @pl.when(me > 0)
    def _():
        halos[0].wait_recv()

    @pl.when(me < peers - 1)
    def _():
        halos[1].wait_recv()

    left = jnp.where(me > 0, left_ref[...], 0.0)
    right = jnp.where(me < peers - 1, right_ref[...], 0.0)
    lane = iota((sub_rows, lanes), 1)
    wide = jnp.concatenate([template_ref[...], jnp.where(lane < half, right, 0.0)], axis=1)
    wide = pltpu.roll(wide, half, 1)
    first_block = jnp.where(lane < half, pltpu.roll(left, half, 1), wide[:, :lanes])
    for b in range(blocks):
        own = first_block if b == 0 else wide[:, b * lanes : (b + 1) * lanes]
        framed_ref[b, above:below] = own.reshape(below - above, 8, lanes)
    tell_recv()
    if peers != pairs:
        go_recv()

    def one_group(group):
        fit_group(
            group * pairs,
            pairs,
            strip_rows,
            top - half,
            bases,
            me,
            info_ref,
            stamp_r_ref,
            stamp_c_ref,
            framed_ref,
            pixels_ref,
            row_bands_ref,
            col_bands_ref,
            across_ref,
            weight_ref,
            design_ref,
            gram_ref,
            residual_ref,
            go_recv if peers == pairs else lambda: None,
        )

    if peers == pairs:
        one_group(0)
    else:
        pl.loop(0, peers // pairs)(one_group)

    back()
    back_recv()
    strip_hot = jnp.where(slot_down == iota((strips, slots), 1), 1.0, 0.0)
    for r in range(strip_rows):
        out_ref[:, r, :] = exact_dot(
            strip_hot, returned_ref[pl.ds(r, slots, stride=strip_rows), :]
        )

    @pl.when(me < peers - 1)
    def _():
        halos[0].wait_send()

    @pl.when(me > 0)
    def _():
        halos[1].wait_send()

    tell_send()
    go_send()
    back_send()


def on_device(
    template, science, dest, row_offset, col_block, basis_rows, basis_cols, stamp_rows, stamp_cols
):
    peers = lax.axis_size("patch")
    strips, strip_rows, lanes = science.shape
    sub_rows, sub_cols = template.shape
    bases, taps = basis_rows.shape
    pair_rows = CAP * strip_rows
    pairs = math.gcd(peers, 16)
    n_rows = pairs * pair_rows
    padded = up(bases + 2, 8)
    even = up(bases, 2)
    pitch = 2 * lanes // 4 // CAP
    half = (taps - 1) // 2
    tiles = (sub_rows - strip_rows + up(half, 8) - half) // 8 + pitch // 8
    vmem = pl.BlockSpec(memory_space=pltpu.VMEM)
    sems = pltpu.SemaphoreType.DMA
    return pl.pallas_call(
        whole_kernel,
        out_shape=jax.ShapeDtypeStruct(science.shape, F32),
        in_specs=[pl.BlockSpec(memory_space=pltpu.HBM)] * 9,
        out_specs=vmem,
        scratch_shapes=[
            pltpu.VMEM(template.shape, F32),
            pltpu.VMEM(science.shape, F32),
            pltpu.VMEM((1, strips), jnp.int32),
            pltpu.VMEM((1, strips), jnp.int32),
            pltpu.VMEM((1, strips), jnp.int32),
            pltpu.VMEM((taps, bases), F32),
            pltpu.VMEM((taps, bases), F32),
            pltpu.SMEM(stamp_rows.shape, jnp.int32),
            pltpu.SMEM(stamp_cols.shape, jnp.int32),
            pltpu.VMEM((even * pair_rows, lanes), F32),
            pltpu.VMEM((CAP, 8, even * pair_rows, 2 * lanes), BF16),
            pltpu.VMEM((bases, 2 * lanes, 2 * lanes), BF16),
            pltpu.VMEM((bases, n_rows, 2 * lanes), F32),
            pltpu.VMEM((n_rows, lanes), F32),
            pltpu.VMEM((padded * n_rows, lanes), F32),
            pltpu.VMEM((pairs * padded, lanes), F32),
            pltpu.VMEM((sub_cols // lanes + 1, tiles, 8, lanes), F32),
            pltpu.VMEM((sub_rows, lanes), F32),
            pltpu.VMEM((sub_rows, lanes), F32),
            pltpu.VMEM((peers * pair_rows, lanes), F32),
            pltpu.VMEM((peers, 1, lanes), jnp.int32),
            pltpu.VMEM((peers * pair_rows, lanes), F32),
            pltpu.VMEM((peers, 1, lanes), jnp.int32),
            pltpu.VMEM((peers * pair_rows, lanes), F32),
            pltpu.VMEM((peers * pair_rows, lanes), F32),
            sems((1, peers)),
            sems((1, peers)),
            sems((1, peers)),
            sems((1, peers)),
            sems((1, peers)),
            sems((1, peers)),
            sems((2,)),
            sems((2,)),
            sems((9,)),
        ],
        compiler_params=pltpu.CompilerParams(
            collective_id=0, has_side_effects=True, vmem_limit_bytes=62 << 20
        ),
    )(
        template,
        science,
        dest.reshape(1, strips),
        row_offset.reshape(1, strips),
        col_block.reshape(1, strips),
        basis_rows.T,
        basis_cols.T,
        stamp_rows,
        stamp_cols,
    )


def solution(mesh):
    placed = (
        P(None, ("groups", "patch")),
        P(("groups", "patch"), None, None),
        P(("groups", "patch"), None),
        P(("groups", "patch")),
        P(("groups", "patch")),
        P(),
        P(),
        P("groups", None),
        P("groups", None),
    )
    return jax.shard_map(
        on_device,
        mesh=mesh,
        in_specs=placed,
        out_specs=P(("groups", "patch"), None, None),
        check_vma=False,
    )
```
